32 devices in a mesh: seq: 4 (over z), ch: 8 (over y, x, core).
Axes of the slice: x: 2, y: 2, z: 4, core: 2. Of those that a mesh axis runs over, the one named last changes fastest.
Arguments:
- proj: bfloat16 [4, 2048, 3, 8192], P(None, ('seq', 'ch')), may hold values from -6 to 6
- short_w: float32 [3, 3, 8192], P(None, None, 'ch'), may hold values from -3.5 to 3.5
- long_filter: bfloat16 [512, 2048], P('ch'), may hold values from -1 to 1
Outputs:
- hyena_out: bfloat16 [4, 2048, 8192], P(None, ('seq', 'ch'))
The draws below stay inside these ranges and needn't reach their ends.
All inputs are finite; a program needn't handle non-finite values.
Results may differ from the reference program's by a relative error of at most 0.0085.
Values may be sent and summed in bfloat16 or wider, within the bound.
No kernel may reach another device: no remote copies, remote signals or barrier semaphores. Data moves between devices by JAX's collectives and lax.ppermute only.
A program may use at most 448 MiB of HBM per device.

```python
import math
import jax
import jax.numpy as jnp
from jax import lax

D = 8192
GSIZE = 16
KS = 3
SEQS = 4
L = 2048
GROUPS = 512


def draw_long_filter(key, part):
    rate_key, noise_key = jax.random.split(jax.random.fold_in(key, 17))
    spread = jax.random.uniform(rate_key, (GROUPS, 1), jnp.float32)
    slowest = jnp.log(0.02 / L)
    fastest = jnp.log(1.0 / 40.0)
    noise = jax.random.truncated_normal(noise_key, -4.0, 4.0, (GROUPS, L), jnp.float32)
    decay = jnp.exp(slowest + spread * (fastest - slowest))
    positions = jnp.arange(L, dtype=jnp.float32)[None, :]
    normalizer = jnp.sqrt((1.0 - jnp.exp(-2.0 * decay)) / (1.0 - jnp.exp(-2.0 * decay * L)))
    return (noise * jnp.exp(-decay * positions) * normalizer).astype(jnp.bfloat16)


def block_levels(own_key, shape, cuts, low, high):
    gain, own = 1.0, jax.random.fold_in(own_key, 6)
    for dim, parts in cuts:
        draws = jnp.exp(jax.random.uniform(jax.random.fold_in(own, dim), (parts,), jnp.float32, low / len(cuts), high / len(cuts)))
        gain = gain * jnp.repeat(draws, shape[dim] // parts).reshape([-1 if axis == dim else 1 for axis in range(len(shape))])
    return gain


def normal_values(key, shape, deviation, bound, cuts=(), kind=jnp.bfloat16):
    result = jax.random.normal(key, shape, jnp.float32) * deviation
    if len(cuts) > 0:
        result = block_levels(key, shape, cuts, -0.22, 0.18) * result
    return jnp.clip(result, min=-bound, max=bound).astype(kind)


def setup_inputs(seed: int = 0) -> dict:
    seeds = jax.random.split(jax.random.key(seed), 4)
    return {
        "proj": normal_values(seeds[0], (SEQS, L, 3, D), 1.0, 6.0, ((1, 32),)),
        "short_w": normal_values(seeds[1], (KS, 3, D), KS ** -0.5, 3.5, ((2, 8),), jnp.float32),
        "long_filter": draw_long_filter(jax.random.fold_in(seeds[3], 71), 0),
    }


def reference(proj, short_w, long_filter):
    chan_block = math.gcd(D, 512)
    block_count = D // chan_block

    def one_block(block_index):
        first_chan = block_index * chan_block
        source = lax.dynamic_slice_in_dim(proj, first_chan, chan_block, 3).astype(jnp.float32)
        weights = lax.dynamic_slice_in_dim(short_w, first_chan, chan_block, 2).astype(jnp.float32)
        filter_taps = lax.dynamic_slice_in_dim(long_filter, first_chan // GSIZE, chan_block // GSIZE, 0).astype(jnp.float32)
        features = weights[0] * source
        for offset in range(1, KS):
            shifted = jnp.pad(source, ((0, 0), (offset, 0), (0, 0), (0, 0)))[:, :L]
            features = features + weights[offset] * shifted
        queries = features[:, :, 0].astype(jnp.bfloat16)
        product = (features[:, :, 1] * features[:, :, 2]).astype(jnp.bfloat16)
        kernel = jnp.repeat(filter_taps, GSIZE, axis=0).T
        spectrum = jnp.fft.rfft(product.astype(jnp.float32), n=2 * L, axis=1) * jnp.fft.rfft(kernel, n=2 * L, axis=0)[None]
        filtered = jnp.fft.irfft(spectrum, n=2 * L, axis=1)[:, :L]
        return (queries.astype(jnp.float32) * filtered).astype(jnp.bfloat16)

    blocks = lax.map(one_block, jnp.arange(block_count, dtype=jnp.int32))
    return jnp.moveaxis(blocks, 0, 2).reshape(SEQS, L, D)
```

```python
import functools
import math

import jax
import jax.numpy as jnp
from jax import lax
from jax.experimental import pallas as pl
from jax.experimental.pallas import tpu as pltpu
from jax.sharding import PartitionSpec as P

GSIZE = 16
CHUNKS = 1
VMEM = 56 * 1024 * 1024


def from_behind(value, axis, steps):
    count = lax.axis_size(axis)
    first, last = (max(0, -steps), min(count, count - steps))
    return lax.ppermute(value, axis, [(source, source + steps) for source in range(first, last)])


def params(*semantics):
    return pltpu.CompilerParams(dimension_semantics=semantics, vmem_limit_bytes=VMEM)


def filtered_rows(rows, rim, taps):
    rows, rim = rows.astype(jnp.float32), rim.astype(jnp.float32)
    place = lax.broadcasted_iota(jnp.int32, rows.shape, 0)
    total = taps[0:1] * rows
    for offset in range(1, taps.shape[0]):
        shifted = pltpu.roll(rows, offset, 0)
        for row in range(offset):
            source = rim.shape[0] - offset + row
            shifted = jnp.where(place == row, rim[source : source + 1], shifted)
        total = total + taps[offset : offset + 1] * shifted
    return total


def product_kernel(key_ref, value_ref, key_rim, value_rim, key_taps, value_taps, out_ref):
    parts, width = out_ref.shape[0], out_ref.shape[-1]
    for n in range(key_ref.shape[0]):
        for part in range(parts):
            lanes = slice(part * width, (part + 1) * width)
            keys = filtered_rows(key_ref[n, 0, :, lanes], key_rim[n, 0, :, lanes], key_taps[0, :, lanes])
            values = filtered_rows(value_ref[n, 0, :, lanes], value_rim[n, 0, :, lanes], value_taps[0, :, lanes])
            out_ref[part, 0, n] = (keys * values).astype(jnp.bfloat16)


def products(proj, rim, taps, first, count, seq, ch):
    rows, channels = proj.shape[2:]
    block, width = channels // ch, channels // (ch * seq)
    start = first // count

    def of(component, depth):
        return pl.BlockSpec((count, 1, depth, block), lambda j: (start, component, 0, j))

    def tap_of(component):
        return pl.BlockSpec((1, taps.shape[1], block), lambda j: (component, 0, j))

    return pl.pallas_call(
        product_kernel,
        grid=(ch,),
        in_specs=[of(1, rows), of(2, rows), of(1, rim.shape[2]), of(2, rim.shape[2]), tap_of(1), tap_of(2)],
        out_specs=pl.BlockSpec((seq, 1, count, rows, width), lambda j: (0, j, 0, 0, 0)),
        out_shape=jax.ShapeDtypeStruct((seq, ch, count, rows, width), jnp.bfloat16),
        compiler_params=params("arbitrary"),
        cost_estimate=pl.CostEstimate(
            flops=20 * count * rows * channels, bytes_accessed=6 * count * rows * channels, transcendentals=0
        ),
        name="products",
    )(proj, proj, rim, rim, taps, taps)


def queries_kernel(query_ref, query_rim, query_taps, out_ref):
    for n in range(query_ref.shape[0]):
        out_ref[n] = filtered_rows(query_ref[n, 0], query_rim[n, 0], query_taps[0]).astype(jnp.bfloat16)


def short_queries(proj, rim, taps, ch):
    count, _, rows, channels = proj.shape
    block = channels // ch

    def of(depth):
        return pl.BlockSpec((count, 1, depth, block), lambda j: (0, 0, 0, j))

    return pl.pallas_call(
        queries_kernel,
        grid=(ch,),
        in_specs=[of(rows), of(rim.shape[2]), pl.BlockSpec((1, taps.shape[1], block), lambda j: (0, 0, j))],
        out_specs=pl.BlockSpec((count, rows, block), lambda j: (0, 0, j)),
        out_shape=jax.ShapeDtypeStruct((count, rows, channels), jnp.bfloat16),
        compiler_params=params("arbitrary"),
        cost_estimate=pl.CostEstimate(
            flops=8 * count * rows * channels, bytes_accessed=4 * count * rows * channels, transcendentals=0
        ),
        name="queries",
    )(proj, rim, taps)


def toeplitz_kernel(filter_ref, out_ref):
    tile, length = out_ref.shape[1:]
    repeated = jnp.broadcast_to(filter_ref[0], (tile, length))
    skewed = pltpu.roll(repeated, 0, 1, stride=1, stride_axis=0)
    source = lax.broadcasted_iota(jnp.int32, (tile, length), 0)
    target = lax.broadcasted_iota(jnp.int32, (tile, length), 1)
    out_ref[0] = jnp.where(target >= source, skewed, 0.0).astype(jnp.bfloat16)


def toeplitz(filters, tile):
    groups, length = filters.shape
    return pl.pallas_call(
        toeplitz_kernel,
        grid=(groups,),
        in_specs=[pl.BlockSpec((1, 1, length), lambda g: (g, 0, 0))],
        out_specs=pl.BlockSpec((1, tile, length), lambda g: (g, 0, 0)),
        out_shape=jax.ShapeDtypeStruct((groups, tile, length), jnp.bfloat16),
        compiler_params=params("arbitrary"),
        cost_estimate=pl.CostEstimate(
            flops=8 * groups * tile * length, bytes_accessed=2 * groups * tile * length, transcendentals=0
        ),
        name="toeplitz",
    )(filters.astype(jnp.float32).reshape(groups, 1, length))


def conv_kernel(x_ref, table_ref, y_ref, turned, acc, done):
    blocks, count, rows, width = x_ref.shape
    tile, length = table_ref.shape[1:]
    tiles, span = length // tile, tile // rows
    group, strip = pl.program_id(1), count * GSIZE

    @pl.when(group == 0)
    def _():
        for u in range(tiles):
            for n in range(count):
                block = x_ref[u * span : (u + 1) * span, n].reshape(tile, width)
                turned[u * count + n] = block.T

    own = pl.ds(pl.multiple_of(group * GSIZE, GSIZE), GSIZE)
    mine = turned[:, own, :].reshape(tiles * strip, tile)
    for lag in range(tiles):
        part = jnp.dot(
            mine[: (tiles - lag) * strip],
            table_ref[0, :, lag * tile : (lag + 1) * tile],
            preferred_element_type=jnp.float32,
        )
        if lag == 0:
            acc[...] = part
        else:
            acc[lag * strip :] += part
    done[:, own, :] = acc[...].astype(jnp.bfloat16).reshape(tiles * count, GSIZE, tile)

    @pl.when(group == pl.num_programs(1) - 1)
    def _():
        for u in range(tiles):
            for n in range(count):
                block = done[u * count + n].T
                y_ref[u * span : (u + 1) * span, n] = block.reshape(span, rows, width)


def long_conv(x, table):
    blocks, count, rows, channels = x.shape
    groups, tile, length = table.shape
    width = math.gcd(channels, 128)
    per_block, tiles = width // GSIZE, length // tile
    spec = pl.BlockSpec((blocks, count, rows, width), lambda j, g: (0, 0, 0, j))
    return pl.pallas_call(
        conv_kernel,
        grid=(channels // width, per_block),
        in_specs=[spec, pl.BlockSpec((1, tile, length), lambda j, g: (j * per_block + g, 0, 0))],
        out_specs=spec,
        out_shape=jax.ShapeDtypeStruct(x.shape, jnp.bfloat16),
        scratch_shapes=[
            pltpu.VMEM((tiles * count, width, tile), jnp.bfloat16),
            pltpu.VMEM((tiles * count * GSIZE, tile), jnp.float32),
            pltpu.VMEM((tiles * count, width, tile), jnp.bfloat16),
        ],
        compiler_params=params("arbitrary", "arbitrary"),
        cost_estimate=pl.CostEstimate(
            flops=groups * (tiles + 1) * tiles * tile * tile * count * GSIZE,
            bytes_accessed=4 * x.size + 2 * table.size,
            transcendentals=0,
        ),
        name="long_conv",
    )(x, table)


def gate_kernel(query_ref, filtered_ref, out_ref):
    parts, width = filtered_ref.shape[0], filtered_ref.shape[-1]
    for n in range(query_ref.shape[0]):
        for part in range(parts):
            lanes = slice(part * width, (part + 1) * width)
            gated = query_ref[n, :, lanes].astype(jnp.float32) * filtered_ref[part, 0, n].astype(jnp.float32)
            out_ref[n, :, lanes] = gated.astype(jnp.bfloat16)


def gate(queries, filtered):
    seq, ch, count, rows, width = filtered.shape
    channels = queries.shape[-1]
    spec = pl.BlockSpec((count, rows, seq * width), lambda j: (0, 0, j))
    return pl.pallas_call(
        gate_kernel,
        grid=(ch,),
        in_specs=[spec, pl.BlockSpec((seq, 1, count, rows, width), lambda j: (0, j, 0, 0, 0))],
        out_specs=spec,
        out_shape=jax.ShapeDtypeStruct((count, rows, channels), jnp.bfloat16),
        compiler_params=params("arbitrary"),
        cost_estimate=pl.CostEstimate(
            flops=count * rows * channels, bytes_accessed=6 * count * rows * channels, transcendentals=0
        ),
        name="gate",
    )(queries, filtered)


def shards(proj, short_w, long_filter):
    axes = ("seq", "ch")
    seq, ch = lax.axis_size("seq"), lax.axis_size("ch")
    tap_count, (seq_count, rows) = short_w.shape[0], proj.shape[:2]
    length, groups = long_filter.shape[1], long_filter.shape[0] // seq
    tile = min(256, length)
    rim = from_behind(proj[:, rows - (tap_count - 1) :], axes, 1).transpose(0, 2, 1, 3)
    taps = lax.all_gather(short_w, "ch", axis=2, tiled=True).transpose(1, 0, 2)
    turned = proj.transpose(0, 2, 1, 3)
    own = lax.dynamic_slice_in_dim(long_filter, lax.axis_index("seq") * groups, groups, 0)
    table = toeplitz(own, tile)
    queries = short_queries(turned, rim, taps, ch)
    sent = products(turned, rim, taps, 0, seq_count, seq, ch)
    sent = sent.reshape((seq * ch,) + sent.shape[2:])
    arrived = lax.all_to_all(sent, axes, split_axis=0, concat_axis=0, tiled=True)
    filtered = long_conv(arrived, table)
    returned = lax.all_to_all(filtered, axes, split_axis=0, concat_axis=0, tiled=True)
    return gate(queries, returned.reshape((seq, ch) + returned.shape[1:]))


def solution(mesh):
    in_specs = (P(None, ("seq", "ch"), None, None), P(None, None, "ch"), P("ch", None))
    out_specs = P(None, ("seq", "ch"), None)
    return jax.shard_map(shards, mesh=mesh, in_specs=in_specs, out_specs=out_specs, check_vma=False)
```

```python
import functools
import math

import jax
import jax.numpy as jnp
from jax import lax
from jax.experimental import pallas as pl
from jax.experimental.pallas import tpu as pltpu
from jax.sharding import PartitionSpec as P

GSIZE = 16
VMEM = 56 * 1024 * 1024


def from_behind(value, axis, steps):
    count = lax.axis_size(axis)
    first, last = (max(0, -steps), min(count, count - steps))
    return lax.ppermute(value, axis, [(source, source + steps) for source in range(first, last)])


def params(*semantics):
    return pltpu.CompilerParams(dimension_semantics=semantics, vmem_limit_bytes=VMEM)


def filtered_rows(shifted, rows, rim, taps):
    count, reach = rows.shape[0], rim.shape[0]
    rows = rows.astype(jnp.float32)
    shifted[8 : 8 + count] = rows
    shifted[8 - reach : 8] = rim.astype(jnp.float32)
    total = taps[0:1] * rows
    for offset in range(1, reach + 1):
        total = total + taps[offset : offset + 1] * shifted[8 - offset : 8 - offset + count]
    return total


def product_kernel(place_ref, key_ref, value_ref, key_rim, value_rim, key_taps, value_taps, *refs, seq, outs):
    shifted, outs = refs[-1], refs[-1 - outs : -1]
    count, width = key_ref.shape[0], outs[0].shape[-1]
    spans, lane = key_ref.shape[-1] // (seq * width), shifted.shape[-1]
    for n in range(count):
        for span in range(spans):
            for part in range(seq):
                for low in range(0, width, lane):
                    start = (span * seq + part) * width + low
                    if len(outs) > 1 and lane % 128 == 0:
                        start = pl.multiple_of((span * seq + (place_ref[0] ^ part)) * width + low, lane)
                    lanes = pl.ds(start, lane)
                    keys = filtered_rows(
                        shifted.at[0], key_ref[n, 0, :, lanes], key_rim[n, 0, :, lanes], key_taps[0, :, lanes]
                    )
                    values = filtered_rows(
                        shifted.at[1], value_ref[n, 0, :, lanes], value_rim[n, 0, :, lanes], value_taps[0, :, lanes]
                    )
                    product = (keys * values).astype(jnp.bfloat16)
                    if len(outs) == 1:
                        outs[0][span, place_ref[0] ^ part, n, :, low : low + lane] = product
                    elif lane % 128 == 0:
                        outs[part][span, n, :, low : low + lane] = product
                    else:
                        for step in range(seq):

                            @pl.when((place_ref[0] ^ part) == step)
                            def _(step=step, n=n, span=span, low=low, product=product):
                                outs[step][span, n, :, low : low + lane] = product


def products(place, proj, rim, taps, first, count, seq, ch, joined, after=()):
    rows, channels = proj.shape[2:]
    width = channels // (ch * seq)
    spans = math.gcd(ch, 2)
    block, start = spans * seq * width, first // count

    def of(component, depth):
        return pl.BlockSpec((count, 1, depth, block), lambda j, *_: (start, component, 0, j))

    def tap_of(component):
        return pl.BlockSpec((1, taps.shape[1], block), lambda j, *_: (component, 0, j))

    if joined:
        out_specs = [pl.BlockSpec((spans, seq, count, rows, width), lambda j, *_: (j, 0, 0, 0, 0))]
        out_shape = [jax.ShapeDtypeStruct((ch, seq, count, rows, width), jnp.bfloat16)]
    else:
        out_specs = [pl.BlockSpec((spans, count, rows, width), lambda j, *_: (j, 0, 0, 0))] * seq
        out_shape = [jax.ShapeDtypeStruct((ch, count, rows, width), jnp.bfloat16)] * seq
    return pl.pallas_call(
        functools.partial(product_kernel, seq=seq, outs=len(out_shape)),
        grid_spec=pltpu.PrefetchScalarGridSpec(
            num_scalar_prefetch=1,
            grid=(ch // spans,),
            in_specs=[of(1, rows), of(2, rows), of(1, rim.shape[2]), of(2, rim.shape[2]), tap_of(1), tap_of(2)]
            + [pl.BlockSpec(memory_space=pl.ANY)] * len(after),
            out_specs=out_specs,
            scratch_shapes=[pltpu.VMEM((2, rows + 8, math.gcd(width, 128)), jnp.float32)],
        ),
        out_shape=out_shape,
        compiler_params=params("arbitrary"),
        cost_estimate=pl.CostEstimate(
            flops=20 * count * rows * channels, bytes_accessed=6 * count * rows * channels, transcendentals=0
        ),
        name="products",
    )(place, proj, proj, rim, rim, taps, taps, *after)


def queries_kernel(query_ref, query_rim, query_taps, out_ref, shifted):
    lane = shifted.shape[-1]
    for n in range(query_ref.shape[0]):
        for low in range(0, query_ref.shape[-1], lane):
            lanes = slice(low, low + lane)
            total = filtered_rows(shifted, query_ref[n, 0, :, lanes], query_rim[n, 0, :, lanes], query_taps[0, :, lanes])
            out_ref[n, :, lanes] = total.astype(jnp.bfloat16)


def short_queries(proj, rim, taps, ch):
    count, _, rows, channels = proj.shape
    block = channels // ch * math.gcd(ch, 2)

    def of(depth):
        return pl.BlockSpec((count, 1, depth, block), lambda j: (0, 0, 0, j))

    return pl.pallas_call(
        queries_kernel,
        grid=(channels // block,),
        in_specs=[of(rows), of(rim.shape[2]), pl.BlockSpec((1, taps.shape[1], block), lambda j: (0, 0, j))],
        out_specs=pl.BlockSpec((count, rows, block), lambda j: (0, 0, j)),
        out_shape=jax.ShapeDtypeStruct((count, rows, channels), jnp.bfloat16),
        scratch_shapes=[pltpu.VMEM((rows + 8, math.gcd(block, 128)), jnp.float32)],
        compiler_params=params("arbitrary"),
        cost_estimate=pl.CostEstimate(
            flops=8 * count * rows * channels, bytes_accessed=4 * count * rows * channels, transcendentals=0
        ),
        name="queries",
    )(proj, rim, taps)


def build_table(filter_row, table_ref):
    tile, length = table_ref.shape
    skewed = pltpu.roll(jnp.broadcast_to(filter_row, (tile, length)), 0, 1, stride=1, stride_axis=0)
    source = lax.broadcasted_iota(jnp.int32, (tile, tile), 0)
    target = lax.broadcasted_iota(jnp.int32, (tile, tile), 1)
    table_ref[:, :tile] = jnp.where(target >= source, skewed[:, :tile], 0.0).astype(jnp.bfloat16)
    if length > tile:
        table_ref[:, tile:] = skewed[:, tile:].astype(jnp.bfloat16)


def convolve(filter_ref, turned, table, acc, done, count):
    tile, length = table.shape[1:]
    tiles, strip = length // tile, count * GSIZE
    for group in range(table.shape[0]):
        build_table(filter_ref[group], table.at[group])
    for group in range(table.shape[0]):
        own = slice(group * GSIZE, (group + 1) * GSIZE)
        mine = turned[:, own, :].reshape(tiles * strip, tile)
        for lag in range(tiles):
            part = jnp.dot(
                mine[: (tiles - lag) * strip],
                table[group, :, lag * tile : (lag + 1) * tile],
                preferred_element_type=jnp.float32,
            )
            if lag == 0:
                acc[group] = part
            else:
                acc[group, lag * strip :] += part
        done[:, own, :] = acc[group].astype(jnp.bfloat16).reshape(tiles * count, GSIZE, tile)


def pieces_of(tile_index, span, ch):
    first, last, found = tile_index * span, (tile_index + 1) * span, []
    while first < last:
        stop = min(last, (first // ch + 1) * ch)
        found.append((first // ch, first % ch, first % ch + stop - first))
        first = stop
    return found


def conv_kernel(place_ref, *refs, seq, joined):
    turned, table, acc, done, gathered = refs[-5:]
    ch, _, count, rows, width = gathered.shape
    outs = refs[-5 - seq : -5] if joined else refs[-6:-5]
    ins, filter_ref = (refs[:1], refs[1]) if joined else (refs[:seq], refs[seq])
    tile, length = table.shape[1:]
    tiles, span = length // tile, tile // rows
    if joined:
        source = ins[0]
    else:
        source = gathered
        for step in range(seq):
            gathered[:, step] = ins[step][...]
    for u in range(tiles):
        for n in range(count):
            blocks = [
                source[low:high, place_ref[0] ^ z, n].reshape((high - low) * rows, width)
                for z, low, high in pieces_of(u, span, ch)
            ]
            block = blocks[0] if len(blocks) == 1 else jnp.concatenate(blocks, axis=0)
            turned[u * count + n] = block.T
    convolve(filter_ref, turned, table, acc, done, count)
    target = gathered if joined else outs[0]
    for u in range(tiles):
        for n in range(count):
            block, start = done[u * count + n].T, 0
            for z, low, high in pieces_of(u, span, ch):
                stop = start + (high - low) * rows
                target[low:high, place_ref[0] ^ z, n] = block[start:stop].reshape(high - low, rows, width)
                start = stop
    if joined:
        for step in range(seq):
            outs[step][...] = gathered[:, step]


def conv_scratch(count, width, tile, length):
    tiles, groups = length // tile, width // GSIZE
    return [
        pltpu.VMEM((tiles * count, width, tile), jnp.bfloat16),
        pltpu.VMEM((groups, tile, length), jnp.bfloat16),
        pltpu.VMEM((groups, tiles * count * GSIZE, tile), jnp.float32),
        pltpu.VMEM((tiles * count, width, tile), jnp.bfloat16),
    ]


def long_conv(place, pieces, filters, seq, after=()):
    joined = len(pieces) == 1
    ch, (count, rows, channels) = pieces[0].shape[0], pieces[0].shape[-3:]
    groups, _, length = filters.shape
    width, tile = math.gcd(channels, 128), min(256, length)
    tiles = length // tile
    one = pl.BlockSpec((ch, seq, count, rows, width), lambda j, place: (0, 0, 0, 0, j))
    part = pl.BlockSpec((ch, count, rows, width), lambda j, place: (0, 0, 0, j))
    whole_shape = jax.ShapeDtypeStruct((ch, seq, count, rows, channels), jnp.bfloat16)
    part_shape = jax.ShapeDtypeStruct((ch, count, rows, channels), jnp.bfloat16)
    return pl.pallas_call(
        functools.partial(conv_kernel, seq=seq, joined=joined),
        grid_spec=pltpu.PrefetchScalarGridSpec(
            num_scalar_prefetch=1,
            grid=(channels // width,),
            in_specs=([one] if joined else [part] * seq)
            + [pl.BlockSpec((width // GSIZE, 1, length), lambda j, place: (j, 0, 0))]
            + [pl.BlockSpec(memory_space=pl.ANY)] * len(after),
            out_specs=[part] * seq if joined else [one],
            scratch_shapes=conv_scratch(count, width, tile, length)
            + [pltpu.VMEM((ch, seq, count, rows, width), jnp.bfloat16)],
        ),
        out_shape=[part_shape] * seq if joined else [whole_shape],
        compiler_params=params("arbitrary"),
        cost_estimate=pl.CostEstimate(
            flops=groups * (tiles + 1) * tiles * tile * tile * count * GSIZE,
            bytes_accessed=4 * ch * seq * count * rows * channels,
            transcendentals=0,
        ),
        name="long_conv",
    )(place, *pieces, filters, *after)


def join_kernel(*refs, seq):
    for step in range(seq):
        refs[-1][:, step] = refs[step][...]


def join(pieces, after=()):
    seq, (ch, count, rows, width) = len(pieces), pieces[0].shape
    spans = math.gcd(ch, 4)
    return pl.pallas_call(
        functools.partial(join_kernel, seq=seq),
        grid=(ch // spans,),
        in_specs=[pl.BlockSpec((spans, count, rows, width), lambda j: (j, 0, 0, 0))] * seq
        + [pl.BlockSpec(memory_space=pl.ANY)] * len(after),
        out_specs=pl.BlockSpec((spans, seq, count, rows, width), lambda j: (j, 0, 0, 0, 0)),
        out_shape=jax.ShapeDtypeStruct((ch, seq, count, rows, width), jnp.bfloat16),
        compiler_params=params("arbitrary"),
        cost_estimate=pl.CostEstimate(flops=0, bytes_accessed=4 * seq * pieces[0].size, transcendentals=0),
        name="join",
    )(*pieces, *after)


def split_kernel(whole_ref, *refs, seq):
    for step in range(seq):
        refs[step - seq][...] = whole_ref[:, step]


def split(whole, after=()):
    ch, seq, count, rows, width = whole.shape
    spans = math.gcd(ch, 4)
    return pl.pallas_call(
        functools.partial(split_kernel, seq=seq),
        grid=(ch // spans,),
        in_specs=[pl.BlockSpec((spans, seq, count, rows, width), lambda j: (j, 0, 0, 0, 0))]
        + [pl.BlockSpec(memory_space=pl.ANY)] * len(after),
        out_specs=[pl.BlockSpec((spans, count, rows, width), lambda j: (j, 0, 0, 0))] * seq,
        out_shape=[jax.ShapeDtypeStruct((ch, count, rows, width), jnp.bfloat16)] * seq,
        compiler_params=params("arbitrary"),
        cost_estimate=pl.CostEstimate(flops=0, bytes_accessed=4 * whole.size, transcendentals=0),
        name="split",
    )(whole, *after)


def gate_kernel(place_ref, query_ref, *refs, seq, joined):
    out_ref = refs[-1]
    rows, width = out_ref.shape[1], refs[0].shape[-1]
    for home in range(1 if joined else seq):

        def gated(home=home):
            for n in range(query_ref.shape[0]):
                for span in range(refs[0].shape[0]):
                    for part in range(seq):
                        start = (span * seq + part) * width
                        lanes = slice(start, start + width)
                        if joined:
                            filtered = refs[0][span, place_ref[0] ^ part, n]
                        else:
                            filtered = refs[home ^ part][span, n]
                        value = query_ref[n, :, lanes].astype(jnp.float32) * filtered.astype(jnp.float32)
                        out_ref[n, :, lanes] = value.astype(jnp.bfloat16)

        if joined:
            gated()
        else:
            pl.when(place_ref[0] == home)(gated)


def gate(place, queries, pieces, first, seq):
    joined = len(pieces) == 1
    ch, (count, rows, width) = pieces[0].shape[0], pieces[0].shape[-3:]
    spans, start = math.gcd(ch, 2), first // count
    spec = pl.BlockSpec((count, rows, spans * seq * width), lambda j, place: (start, 0, j))
    one = pl.BlockSpec((spans, seq, count, rows, width), lambda j, place: (j, 0, 0, 0, 0))
    part = pl.BlockSpec((spans, count, rows, width), lambda j, place: (j, 0, 0, 0))
    return pl.pallas_call(
        functools.partial(gate_kernel, seq=seq, joined=joined),
        grid_spec=pltpu.PrefetchScalarGridSpec(
            num_scalar_prefetch=1,
            grid=(ch // spans,),
            in_specs=[spec] + ([one] if joined else [part] * seq),
            out_specs=spec,
        ),
        out_shape=jax.ShapeDtypeStruct(queries.shape, jnp.bfloat16),
        input_output_aliases={1: 0},
        compiler_params=params("arbitrary"),
        cost_estimate=pl.CostEstimate(
            flops=count * rows * queries.shape[-1],
            bytes_accessed=6 * count * rows * queries.shape[-1],
            transcendentals=0,
        ),
        name="gate",
    )(place, queries, *pieces)


def swap(pieces):
    count = lax.axis_size("seq")
    return [
        lax.ppermute(piece, "seq", [(source, source ^ step) for source in range(count)]) if step else piece
        for step, piece in enumerate(pieces)
    ]


def spread(whole):
    return lax.all_to_all(whole, "ch", split_axis=0, concat_axis=0, tiled=True)


def staged(times, place, step, *arrays):
    def round_of(_, held):
        return held[0] + 1, *step(held[0], *held[1:])

    return lax.fori_loop(0, times, round_of, (place, *arrays))[1:]


def shards(proj, short_w, long_filter):
    seq, ch = lax.axis_size("seq"), lax.axis_size("ch")
    tap_count, (seq_count, rows) = short_w.shape[0], proj.shape[:2]
    length, groups = long_filter.shape[1], long_filter.shape[0] // seq
    half = seq_count // 2
    place = lax.axis_index("seq").astype(jnp.int32).reshape(1)
    once = jnp.minimum(lax.axis_index("seq") + 1, 1)
    rim = from_behind(proj[:, rows - (tap_count - 1) :], ("seq", "ch"), 1).transpose(0, 2, 1, 3)
    taps = lax.all_gather(short_w, "ch", axis=2, tiled=True).transpose(1, 0, 2)
    turned = proj.transpose(0, 2, 1, 3)
    own = lax.dynamic_slice_in_dim(long_filter, place[0] * groups, groups, 0)
    filters = own.astype(jnp.float32).reshape(groups, 1, length)

    first = products(place, turned, rim, taps, 0, half, seq, ch, False)
    begun = first[0]

    def second_out(place, *held):
        (second,) = products(place, turned, rim, taps, half, half, seq, ch, True, after=[begun])
        return split(spread(second))

    second = staged(once, place, second_out, *[jnp.zeros_like(begun)] * seq)
    second_sent = second[0]

    def first_turn(place, *first):
        return long_conv(place, [spread(join(first, after=[place, second_sent]))], filters, seq)

    first = staged(once, place, first_turn, *swap(first))
    first_sent = first[0]

    def second_turn(place, *second):
        (second,) = long_conv(place, second, filters, seq, after=[first_sent])
        return split(spread(second))

    second = staged(once, place, second_turn, *swap(second))
    second_back = second[0]
    queries = short_queries(turned, rim, taps, ch)

    def first_gate(place, queries, *first):
        return gate(place, queries, [spread(join(first, after=[place, second_back]))], 0, seq), *first

    out = staged(once, place, first_gate, queries, *swap(first))[0]
    return gate(place, out, swap(second), half, seq)


def solution(mesh):
    in_specs = (P(None, ("seq", "ch"), None, None), P(None, None, "ch"), P("ch", None))
    out_specs = P(None, ("seq", "ch"), None)
    return jax.shard_map(shards, mesh=mesh, in_specs=in_specs, out_specs=out_specs, check_vma=False)
```

```python
import functools
import math

import jax
import jax.numpy as jnp
from jax import lax
from jax.experimental import pallas as pl
from jax.experimental.pallas import tpu as pltpu
from jax.sharding import PartitionSpec as P

GSIZE = 16
MIB = 1024 * 1024


def from_behind(value, axis, steps):
    count = lax.axis_size(axis)
    first, last = (max(0, -steps), min(count, count - steps))
    return lax.ppermute(value, axis, [(source, source + steps) for source in range(first, last)])


def params(mib, *semantics):
    return pltpu.CompilerParams(dimension_semantics=semantics, vmem_limit_bytes=mib * MIB)


def filtered_rows(shifted, rows, rim, taps):
    count, reach = rows.shape[0], rim.shape[0]
    rows = rows.astype(jnp.float32)
    shifted[8 : 8 + count] = rows
    shifted[8 - reach : 8] = rim.astype(jnp.float32)
    total = taps[0:1] * rows
    for offset in range(1, reach + 1):
        total = total + taps[offset : offset + 1] * shifted[8 - offset : 8 - offset + count]
    return total


def product_kernel(place_ref, key_ref, value_ref, key_rim, value_rim, taps_ref, *refs, seq, outs):
    shifted, outs = refs[-1], refs[-1 - outs : -1]
    count, width = key_ref.shape[0], outs[0].shape[-1]
    spans, lane = key_ref.shape[-1] // (seq * width), shifted.shape[-1]
    for n in range(count):
        for span in range(spans):
            for part in range(seq):
                for low in range(0, width, lane):
                    start = (span * seq + part) * width + low
                    if len(outs) > 1 and lane % 128 == 0:
                        start = pl.multiple_of((span * seq + (place_ref[0] ^ part)) * width + low, lane)
                    lanes = pl.ds(start, lane)
                    keys = filtered_rows(
                        shifted.at[0], key_ref[n, 0, :, lanes], key_rim[n, 0, :, lanes], taps_ref[:, 1, lanes]
                    )
                    values = filtered_rows(
                        shifted.at[1], value_ref[n, 0, :, lanes], value_rim[n, 0, :, lanes], taps_ref[:, 2, lanes]
                    )
                    product = (keys * values).astype(jnp.bfloat16)
                    if len(outs) == 1:
                        outs[0][span, place_ref[0] ^ part, n, :, low : low + lane] = product
                    elif lane % 128 == 0:
                        outs[part][span, n, :, low : low + lane] = product
                    else:
                        for step in range(seq):

                            @pl.when((place_ref[0] ^ part) == step)
                            def _(step=step, n=n, span=span, low=low, product=product):
                                outs[step][span, n, :, low : low + lane] = product


def products(place, proj, rim, taps, first, count, seq, ch, joined, after=()):
    rows, channels = proj.shape[2:]
    width = channels // (ch * seq)
    spans = math.gcd(ch, 2)
    block, start = spans * seq * width, first // count

    def of(component, depth):
        return pl.BlockSpec((count, 1, depth, block), lambda j, *_: (start, component, 0, j))

    if joined:
        out_specs = [pl.BlockSpec((spans, seq, count, rows, width), lambda j, *_: (j, 0, 0, 0, 0))]
        out_shape = [jax.ShapeDtypeStruct((ch, seq, count, rows, width), jnp.bfloat16)]
    else:
        out_specs = [pl.BlockSpec((spans, count, rows, width), lambda j, *_: (j, 0, 0, 0))] * seq
        out_shape = [jax.ShapeDtypeStruct((ch, count, rows, width), jnp.bfloat16)] * seq
    return pl.pallas_call(
        functools.partial(product_kernel, seq=seq, outs=len(out_shape)),
        grid_spec=pltpu.PrefetchScalarGridSpec(
            num_scalar_prefetch=1,
            grid=(ch // spans,),
            in_specs=[of(1, rows), of(2, rows), of(1, rim.shape[2]), of(2, rim.shape[2])]
            + [pl.BlockSpec(taps.shape[:2] + (block,), lambda j, *_: (0, 0, j))]
            + [pl.BlockSpec(memory_space=pl.ANY)] * len(after),
            out_specs=out_specs,
            scratch_shapes=[pltpu.VMEM((2, rows + 8, math.gcd(width, 128)), jnp.float32)],
        ),
        out_shape=out_shape,
        compiler_params=params(8, "arbitrary"),
        cost_estimate=pl.CostEstimate(
            flops=20 * count * rows * channels, bytes_accessed=6 * count * rows * channels, transcendentals=0
        ),
        name="products",
    )(place, proj, proj, rim, rim, taps, *after)


def queries_kernel(query_ref, query_rim, query_taps, *refs):
    out_ref, shifted = refs[-2:]
    lane = shifted.shape[-1]
    for n in range(query_ref.shape[0]):
        for low in range(0, query_ref.shape[-1], lane):
            lanes = slice(low, low + lane)
            total = filtered_rows(shifted, query_ref[n, 0, :, lanes], query_rim[n, 0, :, lanes], query_taps[:, 0, lanes])
            out_ref[n, :, lanes] = total.astype(jnp.bfloat16)


def short_queries(proj, rim, taps, ch, after=()):
    count, _, rows, channels = proj.shape
    block = channels // ch * math.gcd(ch, 2)

    def of(depth):
        return pl.BlockSpec((count, 1, depth, block), lambda j: (0, 0, 0, j))

    return pl.pallas_call(
        queries_kernel,
        grid=(channels // block,),
        in_specs=[of(rows), of(rim.shape[2]), pl.BlockSpec(taps.shape[:2] + (block,), lambda j: (0, 0, j))]
        + [pl.BlockSpec(memory_space=pl.ANY)] * len(after),
        out_specs=pl.BlockSpec((count, rows, block), lambda j: (0, 0, j)),
        out_shape=jax.ShapeDtypeStruct((count, rows, channels), jnp.bfloat16),
        scratch_shapes=[pltpu.VMEM((rows + 8, math.gcd(block, 128)), jnp.float32)],
        compiler_params=params(8, "arbitrary"),
        cost_estimate=pl.CostEstimate(
            flops=8 * count * rows * channels, bytes_accessed=4 * count * rows * channels, transcendentals=0
        ),
        name="queries",
    )(proj, rim, taps, *after)


def build_table(filter_row, table_ref):
    tile, length = table_ref.shape
    skewed = pltpu.roll(jnp.broadcast_to(filter_row, (tile, length)), 0, 1, stride=1, stride_axis=0)
    source = lax.broadcasted_iota(jnp.int32, (tile, tile), 0)
    target = lax.broadcasted_iota(jnp.int32, (tile, tile), 1)
    table_ref[:, :tile] = jnp.where(target >= source, skewed[:, :tile], 0.0).astype(jnp.bfloat16)
    if length > tile:
        table_ref[:, tile:] = skewed[:, tile:].astype(jnp.bfloat16)


def convolve(filter_ref, turned, table, acc, done, count):
    tile, length = table.shape[1:]
    tiles, strip = length // tile, count * GSIZE
    for group in range(table.shape[0]):
        build_table(filter_ref[group], table.at[group])
    for group in range(table.shape[0]):
        own = slice(group * GSIZE, (group + 1) * GSIZE)
        mine = turned[:, own, :].reshape(tiles * strip, tile)
        for lag in range(tiles):
            part = jnp.dot(
                mine[: (tiles - lag) * strip],
                table[group, :, lag * tile : (lag + 1) * tile],
                preferred_element_type=jnp.float32,
            )
            if lag == 0:
                acc[group] = part
            else:
                acc[group, lag * strip :] += part
        done[:, own, :] = acc[group].astype(jnp.bfloat16).reshape(tiles * count, GSIZE, tile)


def pieces_of(tile_index, span, ch):
    first, last, found = tile_index * span, (tile_index + 1) * span, []
    while first < last:
        stop = min(last, (first // ch + 1) * ch)
        found.append((first // ch, first % ch, first % ch + stop - first))
        first = stop
    return found


def conv_kernel(place_ref, *refs, seq, joined):
    turned, table, acc, done, gathered = refs[-5:]
    ch, _, count, rows, width = gathered.shape
    outs = refs[-5 - seq : -5] if joined else refs[-6:-5]
    ins, filter_ref = (refs[:1], refs[1]) if joined else (refs[:seq], refs[seq])
    tile, length = table.shape[1:]
    tiles, span = length // tile, tile // rows
    if joined:
        source = ins[0]
    else:
        source = gathered
        for step in range(seq):
            gathered[:, step] = ins[step][...]
    for u in range(tiles):
        for n in range(count):
            blocks = [
                source[low:high, place_ref[0] ^ z, n].reshape((high - low) * rows, width)
                for z, low, high in pieces_of(u, span, ch)
            ]
            block = blocks[0] if len(blocks) == 1 else jnp.concatenate(blocks, axis=0)
            turned[u * count + n] = block.T
    convolve(filter_ref, turned, table, acc, done, count)
    target = gathered if joined else outs[0]
    for u in range(tiles):
        for n in range(count):
            block, start = done[u * count + n].T, 0
            for z, low, high in pieces_of(u, span, ch):
                stop = start + (high - low) * rows
                target[low:high, place_ref[0] ^ z, n] = block[start:stop].reshape(high - low, rows, width)
                start = stop
    if joined:
        for step in range(seq):
            outs[step][...] = gathered[:, step]


def conv_scratch(count, width, tile, length):
    tiles, groups = length // tile, width // GSIZE
    return [
        pltpu.VMEM((tiles * count, width, tile), jnp.bfloat16),
        pltpu.VMEM((groups, tile, length), jnp.bfloat16),
        pltpu.VMEM((groups, tiles * count * GSIZE, tile), jnp.float32),
        pltpu.VMEM((tiles * count, width, tile), jnp.bfloat16),
    ]


def long_conv(place, pieces, filters, seq, after=()):
    joined = len(pieces) == 1
    ch, (count, rows, channels) = pieces[0].shape[0], pieces[0].shape[-3:]
    groups, _, length = filters.shape
    width, tile = math.gcd(channels, 128), min(256, length)
    tiles = length // tile
    one = pl.BlockSpec((ch, seq, count, rows, width), lambda j, place: (0, 0, 0, 0, j))
    part = pl.BlockSpec((ch, count, rows, width), lambda j, place: (0, 0, 0, j))
    whole_shape = jax.ShapeDtypeStruct((ch, seq, count, rows, channels), jnp.bfloat16)
    part_shape = jax.ShapeDtypeStruct((ch, count, rows, channels), jnp.bfloat16)
    return pl.pallas_call(
        functools.partial(conv_kernel, seq=seq, joined=joined),
        grid_spec=pltpu.PrefetchScalarGridSpec(
            num_scalar_prefetch=1,
            grid=(channels // width,),
            in_specs=([one] if joined else [part] * seq)
            + [pl.BlockSpec((width // GSIZE, 1, length), lambda j, place: (j, 0, 0))]
            + [pl.BlockSpec(memory_space=pl.ANY)] * len(after),
            out_specs=[part] * seq if joined else [one],
            scratch_shapes=conv_scratch(count, width, tile, length)
            + [pltpu.VMEM((ch, seq, count, rows, width), jnp.bfloat16)],
        ),
        out_shape=[part_shape] * seq if joined else [whole_shape],
        compiler_params=params(32, "arbitrary"),
        cost_estimate=pl.CostEstimate(
            flops=groups * (tiles + 1) * tiles * tile * tile * count * GSIZE,
            bytes_accessed=4 * ch * seq * count * rows * channels,
            transcendentals=0,
        ),
        name="long_conv",
    )(place, *pieces, filters, *after)


def join_kernel(*refs, seq):
    for step in range(seq):
        refs[-1][:, step] = refs[step][...]


def join(pieces, after=()):
    seq, (ch, count, rows, width) = len(pieces), pieces[0].shape
    spans = math.gcd(ch, 4)
    return pl.pallas_call(
        functools.partial(join_kernel, seq=seq),
        grid=(ch // spans,),
        in_specs=[pl.BlockSpec((spans, count, rows, width), lambda j: (j, 0, 0, 0))] * seq
        + [pl.BlockSpec(memory_space=pl.ANY)] * len(after),
        out_specs=pl.BlockSpec((spans, seq, count, rows, width), lambda j: (j, 0, 0, 0, 0)),
        out_shape=jax.ShapeDtypeStruct((ch, seq, count, rows, width), jnp.bfloat16),
        compiler_params=params(8, "arbitrary"),
        cost_estimate=pl.CostEstimate(flops=0, bytes_accessed=4 * seq * pieces[0].size, transcendentals=0),
        name="join",
    )(*pieces, *after)


def split_kernel(whole_ref, *refs, seq):
    for step in range(seq):
        refs[step - seq][...] = whole_ref[:, step]


def split(whole, after=()):
    ch, seq, count, rows, width = whole.shape
    spans = math.gcd(ch, 4)
    return pl.pallas_call(
        functools.partial(split_kernel, seq=seq),
        grid=(ch // spans,),
        in_specs=[pl.BlockSpec((spans, seq, count, rows, width), lambda j: (j, 0, 0, 0, 0))]
        + [pl.BlockSpec(memory_space=pl.ANY)] * len(after),
        out_specs=[pl.BlockSpec((spans, count, rows, width), lambda j: (j, 0, 0, 0))] * seq,
        out_shape=[jax.ShapeDtypeStruct((ch, count, rows, width), jnp.bfloat16)] * seq,
        compiler_params=params(8, "arbitrary"),
        cost_estimate=pl.CostEstimate(flops=0, bytes_accessed=4 * whole.size, transcendentals=0),
        name="split",
    )(whole, *after)


def gate_kernel(place_ref, query_ref, *refs, seq, joined):
    out_ref = refs[-1]
    rows, width = out_ref.shape[1], refs[0].shape[-1]
    for home in range(1 if joined else seq):

        def gated(home=home):
            for n in range(query_ref.shape[0]):
                for span in range(refs[0].shape[0]):
                    for part in range(seq):
                        start = (span * seq + part) * width
                        lanes = slice(start, start + width)
                        if joined:
                            filtered = refs[0][span, place_ref[0] ^ part, n]
                        else:
                            filtered = refs[home ^ part][span, n]
                        value = query_ref[n, :, lanes].astype(jnp.float32) * filtered.astype(jnp.float32)
                        out_ref[n, :, lanes] = value.astype(jnp.bfloat16)

        if joined:
            gated()
        else:
            pl.when(place_ref[0] == home)(gated)


def gate(place, queries, pieces, first, seq):
    joined = len(pieces) == 1
    ch, (count, rows, width) = pieces[0].shape[0], pieces[0].shape[-3:]
    spans, start = math.gcd(ch, 2), first // count
    spec = pl.BlockSpec((count, rows, spans * seq * width), lambda j, place: (start, 0, j))
    one = pl.BlockSpec((spans, seq, count, rows, width), lambda j, place: (j, 0, 0, 0, 0))
    part = pl.BlockSpec((spans, count, rows, width), lambda j, place: (j, 0, 0, 0))
    return pl.pallas_call(
        functools.partial(gate_kernel, seq=seq, joined=joined),
        grid_spec=pltpu.PrefetchScalarGridSpec(
            num_scalar_prefetch=1,
            grid=(ch // spans,),
            in_specs=[spec] + ([one] if joined else [part] * seq),
            out_specs=spec,
        ),
        out_shape=jax.ShapeDtypeStruct(queries.shape, jnp.bfloat16),
        input_output_aliases={1: 0},
        compiler_params=params(8, "arbitrary"),
        cost_estimate=pl.CostEstimate(
            flops=count * rows * queries.shape[-1],
            bytes_accessed=6 * count * rows * queries.shape[-1],
            transcendentals=0,
        ),
        name="gate",
    )(place, queries, *pieces)


def swap(pieces):
    count = lax.axis_size("seq")
    return [
        lax.ppermute(piece, "seq", [(source, source ^ step) for source in range(count)]) if step else piece
        for step, piece in enumerate(pieces)
    ]


def spread(whole):
    return lax.all_to_all(whole, "ch", split_axis=0, concat_axis=0, tiled=True)


def vacant_kernel(*refs):
    pass


def vacant(*arrays):
    return pl.pallas_call(
        vacant_kernel,
        out_specs=[pl.BlockSpec(memory_space=pl.ANY)] * len(arrays),
        out_shape=[jax.ShapeDtypeStruct(array.shape, array.dtype) for array in arrays],
        name="vacant",
    )()


def staged(times, place, step, *arrays):
    def round_of(_, held):
        return held[0] + 1, *step(held[0], *held[1:])

    return lax.fori_loop(0, times, round_of, (place, *arrays))[1:]


def shards(proj, short_w, long_filter):
    seq, ch = lax.axis_size("seq"), lax.axis_size("ch")
    tap_count, (seq_count, rows) = short_w.shape[0], proj.shape[:2]
    length, groups = long_filter.shape[1], long_filter.shape[0] // seq
    half = seq_count // 2
    place = lax.axis_index("seq").astype(jnp.int32).reshape(1)
    once = jnp.minimum(lax.axis_index("seq") + 1, 1)
    rim = from_behind(proj[:, rows - (tap_count - 1) :], ("seq", "ch"), 1).transpose(0, 2, 1, 3)
    taps = lax.all_gather(short_w, "ch", axis=2, tiled=True)
    turned = proj.transpose(0, 2, 1, 3)
    own = lax.dynamic_slice_in_dim(long_filter, place[0] * groups, groups, 0)
    filters = own.astype(jnp.float32).reshape(groups, 1, length)

    first = products(place, turned, rim, taps, 0, half, seq, ch, False)
    begun = first[0]

    def second_out(place, *held):
        (second,) = products(place, turned, rim, taps, half, half, seq, ch, True, after=[begun, place])
        queries = short_queries(turned, rim, taps, ch, after=[place])
        return queries, *split(spread(second))

    shape = jax.ShapeDtypeStruct((seq_count, rows, proj.shape[3]), proj.dtype)
    queries, *second = staged(once, place, second_out, *vacant(shape, *first))
    second_sent = second[0]

    def first_turn(place, *first):
        return long_conv(place, [spread(join(first, after=[place, second_sent]))], filters, seq)

    first = staged(once, place, first_turn, *swap(first))
    first_sent = first[0]

    def second_turn(place, *second):
        (second,) = long_conv(place, second, filters, seq, after=[first_sent])
        return split(spread(second))

    second = staged(once, place, second_turn, *swap(second))
    second_back = second[0]

    def first_gate(place, queries, *first):
        return gate(place, queries, [spread(join(first, after=[place, second_back]))], 0, seq), *first

    out = staged(once, place, first_gate, queries, *swap(first))[0]
    return gate(place, out, swap(second), half, seq)


def solution(mesh):
    in_specs = (P(None, ("seq", "ch"), None, None), P(None, None, "ch"), P("ch", None))
    out_specs = P(None, ("seq", "ch"), None)
    return jax.shard_map(shards, mesh=mesh, in_specs=in_specs, out_specs=out_specs, check_vma=False)
```

```python
import functools
import math

import jax
import jax.numpy as jnp
from jax import lax
from jax.experimental import pallas as pl
from jax.experimental.pallas import tpu as pltpu
from jax.sharding import PartitionSpec as P

GSIZE = 16
MIB = 1024 * 1024


def from_behind(value, axis, steps):
    count = lax.axis_size(axis)
    first, last = (max(0, -steps), min(count, count - steps))
    return lax.ppermute(value, axis, [(source, source + steps) for source in range(first, last)])


def params(mib, *semantics):
    return pltpu.CompilerParams(dimension_semantics=semantics, vmem_limit_bytes=mib * MIB)


def filtered_rows(shifted, rows, rim, taps):
    count, reach = rows.shape[0], rim.shape[0]
    rows = rows.astype(jnp.float32)
    shifted[8 : 8 + count] = rows
    shifted[8 - reach : 8] = rim.astype(jnp.float32)
    total = taps[0:1] * rows
    for offset in range(1, reach + 1):
        total = total + taps[offset : offset + 1] * shifted[8 - offset : 8 - offset + count]
    return total


def product_kernel(place_ref, *refs, seq, outs):
    if outs == 1:
        product_body(place_ref[0], *refs, seq=seq, outs=outs)
        return
    for home in range(seq):
        pl.when(place_ref[0] == home)(functools.partial(product_body, home, *refs, seq=seq, outs=outs))


def product_body(place, key_ref, value_ref, key_rim, value_rim, taps_ref, *refs, seq, outs):
    shifted, outs = refs[-1], refs[-1 - outs : -1]
    count, width = key_ref.shape[0], outs[0].shape[-1]
    spans, lane = key_ref.shape[-1] // (seq * width), shifted.shape[-1]
    for span in range(spans):
        for part in range(seq):
            for low in range(0, width, lane):
                start = (span * seq + part) * width + low
                lanes = slice(start, start + lane)
                key_taps, value_taps = taps_ref[:, 1, lanes], taps_ref[:, 2, lanes]
                for n in range(count):
                    keys = filtered_rows(shifted.at[2 * n], key_ref[n, 0, :, lanes], key_rim[n, 0, :, lanes], key_taps)
                    values = filtered_rows(
                        shifted.at[2 * n + 1], value_ref[n, 0, :, lanes], value_rim[n, 0, :, lanes], value_taps
                    )
                    product = (keys * values).astype(jnp.bfloat16)
                    if len(outs) == 1:
                        outs[0][span, place ^ part, n, :, low : low + lane] = product
                    else:
                        outs[place ^ part][span, n, :, low : low + lane] = product


def products(place, proj, rim, taps, first, count, seq, ch, joined, after=()):
    rows, channels = proj.shape[2:]
    width = channels // (ch * seq)
    spans = math.gcd(ch, 8)
    block = spans * seq * width

    def of(component, depth):
        return pl.BlockSpec((1, 1, depth, block), lambda n, j, *_: (first + n, component, 0, j))

    if joined:
        out_specs = [pl.BlockSpec((spans, seq, 1, rows, width), lambda n, j, *_: (j, 0, n, 0, 0))]
        out_shape = [jax.ShapeDtypeStruct((ch, seq, count, rows, width), jnp.bfloat16)]
    else:
        out_specs = [pl.BlockSpec((spans, 1, rows, width), lambda n, j, *_: (j, n, 0, 0))] * seq
        out_shape = [jax.ShapeDtypeStruct((ch, count, rows, width), jnp.bfloat16)] * seq
    return pl.pallas_call(
        functools.partial(product_kernel, seq=seq, outs=len(out_shape)),
        grid_spec=pltpu.PrefetchScalarGridSpec(
            num_scalar_prefetch=1,
            grid=(count, ch // spans),
            in_specs=[of(1, rows), of(2, rows), of(1, rim.shape[2]), of(2, rim.shape[2])]
            + [pl.BlockSpec(taps.shape[:2] + (block,), lambda n, j, *_: (0, 0, j))]
            + [pl.BlockSpec(memory_space=pl.ANY)] * len(after),
            out_specs=out_specs,
            scratch_shapes=[pltpu.VMEM((2 * count, rows + 8, math.gcd(width, 128)), jnp.float32)],
        ),
        out_shape=out_shape,
        compiler_params=params(14, "arbitrary", "arbitrary"),
        cost_estimate=pl.CostEstimate(
            flops=20 * count * rows * channels, bytes_accessed=6 * count * rows * channels, transcendentals=0
        ),
        name="products",
    )(place, proj, proj, rim, rim, taps, *after)


def queries_kernel(query_ref, query_rim, query_taps, *refs):
    out_ref, shifted = refs[-2:]
    lane = shifted.shape[-1]
    for low in range(0, query_ref.shape[-1], lane):
        lanes = slice(low, low + lane)
        taps = query_taps[:, 0, lanes]
        for n in range(query_ref.shape[0]):
            total = filtered_rows(shifted.at[n], query_ref[n, 0, :, lanes], query_rim[n, 0, :, lanes], taps)
            out_ref[n, :, lanes] = total.astype(jnp.bfloat16)


def short_queries(proj, rim, taps, ch, after=()):
    count, _, rows, channels = proj.shape
    block = channels // ch * math.gcd(ch, 2)

    def of(depth):
        return pl.BlockSpec((count, 1, depth, block), lambda j: (0, 0, 0, j))

    return pl.pallas_call(
        queries_kernel,
        grid=(channels // block,),
        in_specs=[of(rows), of(rim.shape[2]), pl.BlockSpec(taps.shape[:2] + (block,), lambda j: (0, 0, j))]
        + [pl.BlockSpec(memory_space=pl.ANY)] * len(after),
        out_specs=pl.BlockSpec((count, rows, block), lambda j: (0, 0, j)),
        out_shape=jax.ShapeDtypeStruct((count, rows, channels), jnp.bfloat16),
        scratch_shapes=[pltpu.VMEM((count, rows + 8, math.gcd(block, 128)), jnp.float32)],
        compiler_params=params(8, "arbitrary"),
        cost_estimate=pl.CostEstimate(
            flops=8 * count * rows * channels, bytes_accessed=4 * count * rows * channels, transcendentals=0
        ),
        name="queries",
    )(proj, rim, taps, *after)


def build_table(filter_row, table_ref):
    tile, length = table_ref.shape
    skewed = pltpu.roll(jnp.broadcast_to(filter_row, (tile, length)), 0, 1, stride=1, stride_axis=0)
    source = lax.broadcasted_iota(jnp.int32, (tile, tile), 0)
    target = lax.broadcasted_iota(jnp.int32, (tile, tile), 1)
    table_ref[:, :tile] = jnp.where(target >= source, skewed[:, :tile], 0.0).astype(jnp.bfloat16)
    if length > tile:
        table_ref[:, tile:] = skewed[:, tile:].astype(jnp.bfloat16)


def convolve(filter_ref, turned, table, acc, done, count):
    tile, length = table.shape[1:]
    tiles, strip = length // tile, count * GSIZE
    for group in range(table.shape[0]):
        build_table(filter_ref[group], table.at[group])
    for group in range(table.shape[0]):
        own = slice(group * GSIZE, (group + 1) * GSIZE)
        mine = turned[:, own, :].reshape(tiles * strip, tile)
        for lag in range(tiles):
            part = jnp.dot(
                mine[: (tiles - lag) * strip],
                table[group, :, lag * tile : (lag + 1) * tile],
                preferred_element_type=jnp.float32,
            )
            if lag == 0:
                acc[group] = part
            else:
                acc[group, lag * strip :] += part
        done[:, own, :] = acc[group].astype(jnp.bfloat16).reshape(tiles * count, GSIZE, tile)


def pieces_of(tile_index, span, ch):
    first, last, found = tile_index * span, (tile_index + 1) * span, []
    while first < last:
        stop = min(last, (first // ch + 1) * ch)
        found.append((first // ch, first % ch, first % ch + stop - first))
        first = stop
    return found


def conv_kernel(place_ref, *refs, seq, joined):
    turned, table, acc, done, gathered = refs[-5:]
    ch, _, count, rows, width = gathered.shape
    outs = refs[-5 - seq : -5] if joined else refs[-6:-5]
    ins, filter_ref = (refs[:1], refs[1]) if joined else (refs[:seq], refs[seq])
    tile, length = table.shape[1:]
    tiles, span = length // tile, tile // rows
    if joined:
        source = ins[0]
    else:
        source = gathered
        for step in range(seq):
            gathered[:, step] = ins[step][...]
    for u in range(tiles):
        for n in range(count):
            blocks = [
                source[low:high, place_ref[0] ^ z, n].reshape((high - low) * rows, width)
                for z, low, high in pieces_of(u, span, ch)
            ]
            block = blocks[0] if len(blocks) == 1 else jnp.concatenate(blocks, axis=0)
            turned[u * count + n] = block.T
    convolve(filter_ref, turned, table, acc, done, count)
    target = gathered if joined else outs[0]
    for u in range(tiles):
        for n in range(count):
            block, start = done[u * count + n].T, 0
            for z, low, high in pieces_of(u, span, ch):
                stop = start + (high - low) * rows
                target[low:high, place_ref[0] ^ z, n] = block[start:stop].reshape(high - low, rows, width)
                start = stop
    if joined:
        for step in range(seq):
            outs[step][...] = gathered[:, step]


def conv_scratch(count, width, tile, length):
    tiles, groups = length // tile, width // GSIZE
    return [
        pltpu.VMEM((tiles * count, width, tile), jnp.bfloat16),
        pltpu.VMEM((groups, tile, length), jnp.bfloat16),
        pltpu.VMEM((groups, tiles * count * GSIZE, tile), jnp.float32),
        pltpu.VMEM((tiles * count, width, tile), jnp.bfloat16),
    ]


def long_conv(place, pieces, filters, seq, after=()):
    joined = len(pieces) == 1
    ch, (count, rows, channels) = pieces[0].shape[0], pieces[0].shape[-3:]
    groups, _, length = filters.shape
    width, tile = math.gcd(channels, 128), min(256, length)
    tiles = length // tile
    one = pl.BlockSpec((ch, seq, count, rows, width), lambda j, place: (0, 0, 0, 0, j))
    part = pl.BlockSpec((ch, count, rows, width), lambda j, place: (0, 0, 0, j))
    whole_shape = jax.ShapeDtypeStruct((ch, seq, count, rows, channels), jnp.bfloat16)
    part_shape = jax.ShapeDtypeStruct((ch, count, rows, channels), jnp.bfloat16)
    return pl.pallas_call(
        functools.partial(conv_kernel, seq=seq, joined=joined),
        grid_spec=pltpu.PrefetchScalarGridSpec(
            num_scalar_prefetch=1,
            grid=(channels // width,),
            in_specs=([one] if joined else [part] * seq)
            + [pl.BlockSpec((width // GSIZE, 1, length), lambda j, place: (j, 0, 0))]
            + [pl.BlockSpec(memory_space=pl.ANY)] * len(after),
            out_specs=[part] * seq if joined else [one],
            scratch_shapes=conv_scratch(count, width, tile, length)
            + [pltpu.VMEM((ch, seq, count, rows, width), jnp.bfloat16)],
        ),
        out_shape=[part_shape] * seq if joined else [whole_shape],
        compiler_params=params(32, "arbitrary"),
        cost_estimate=pl.CostEstimate(
            flops=groups * (tiles + 1) * tiles * tile * tile * count * GSIZE,
            bytes_accessed=4 * ch * seq * count * rows * channels,
            transcendentals=0,
        ),
        name="long_conv",
    )(place, *pieces, filters, *after)


def join_kernel(*refs, seq):
    for step in range(seq):
        refs[-1][:, step] = refs[step][...]


def join(pieces, after=()):
    seq, (ch, count, rows, width) = len(pieces), pieces[0].shape
    spans = math.gcd(ch, 4)
    return pl.pallas_call(
        functools.partial(join_kernel, seq=seq),
        grid=(ch // spans,),
        in_specs=[pl.BlockSpec((spans, count, rows, width), lambda j: (j, 0, 0, 0))] * seq
        + [pl.BlockSpec(memory_space=pl.ANY)] * len(after),
        out_specs=pl.BlockSpec((spans, seq, count, rows, width), lambda j: (j, 0, 0, 0, 0)),
        out_shape=jax.ShapeDtypeStruct((ch, seq, count, rows, width), jnp.bfloat16),
        compiler_params=params(8, "arbitrary"),
        cost_estimate=pl.CostEstimate(flops=0, bytes_accessed=4 * seq * pieces[0].size, transcendentals=0),
        name="join",
    )(*pieces, *after)


def split_kernel(whole_ref, *refs, seq):
    for step in range(seq):
        refs[step - seq][...] = whole_ref[:, step]


def split(whole, after=()):
    ch, seq, count, rows, width = whole.shape
    spans = math.gcd(ch, 4)
    return pl.pallas_call(
        functools.partial(split_kernel, seq=seq),
        grid=(ch // spans,),
        in_specs=[pl.BlockSpec((spans, seq, count, rows, width), lambda j: (j, 0, 0, 0, 0))]
        + [pl.BlockSpec(memory_space=pl.ANY)] * len(after),
        out_specs=[pl.BlockSpec((spans, count, rows, width), lambda j: (j, 0, 0, 0))] * seq,
        out_shape=[jax.ShapeDtypeStruct((ch, count, rows, width), jnp.bfloat16)] * seq,
        compiler_params=params(8, "arbitrary"),
        cost_estimate=pl.CostEstimate(flops=0, bytes_accessed=4 * whole.size, transcendentals=0),
        name="split",
    )(whole, *after)


def gate_kernel(place_ref, query_ref, *refs, seq, joined):
    out_ref = refs[-1]
    rows, width = out_ref.shape[1], refs[0].shape[-1]
    for home in range(1 if joined else seq):

        def gated(home=home):
            for n in range(query_ref.shape[0]):
                for span in range(refs[0].shape[0]):
                    for part in range(seq):
                        start = (span * seq + part) * width
                        lanes = slice(start, start + width)
                        if joined:
                            filtered = refs[0][span, place_ref[0] ^ part, n]
                        else:
                            filtered = refs[home ^ part][span, n]
                        value = query_ref[n, :, lanes].astype(jnp.float32) * filtered.astype(jnp.float32)
                        out_ref[n, :, lanes] = value.astype(jnp.bfloat16)

        if joined:
            gated()
        else:
            pl.when(place_ref[0] == home)(gated)


def gate(place, queries, pieces, first, seq):
    joined = len(pieces) == 1
    ch, (count, rows, width) = pieces[0].shape[0], pieces[0].shape[-3:]
    spans, start = math.gcd(ch, 2), first // count
    spec = pl.BlockSpec((count, rows, spans * seq * width), lambda j, place: (start, 0, j))
    one = pl.BlockSpec((spans, seq, count, rows, width), lambda j, place: (j, 0, 0, 0, 0))
    part = pl.BlockSpec((spans, count, rows, width), lambda j, place: (j, 0, 0, 0))
    return pl.pallas_call(
        functools.partial(gate_kernel, seq=seq, joined=joined),
        grid_spec=pltpu.PrefetchScalarGridSpec(
            num_scalar_prefetch=1,
            grid=(ch // spans,),
            in_specs=[spec] + ([one] if joined else [part] * seq),
            out_specs=spec,
        ),
        out_shape=jax.ShapeDtypeStruct(queries.shape, jnp.bfloat16),
        input_output_aliases={1: 0},
        compiler_params=params(8, "arbitrary"),
        cost_estimate=pl.CostEstimate(
            flops=count * rows * queries.shape[-1],
            bytes_accessed=6 * count * rows * queries.shape[-1],
            transcendentals=0,
        ),
        name="gate",
    )(place, queries, *pieces)


def half_gate_kernel(place_ref, queries_ref, *refs, first, half, far):
    pieces, out_ref, query, gated, arrive, leave = refs[:half], *refs[-5:]
    ch, count, _, width = pieces[0].shape
    block = half * width

    def column(c):
        place = c * 2 + (lax.div(place_ref[0], half) ^ int(far))
        return pl.ds(pl.multiple_of(place * block, block), block)

    def inward(c):
        source = queries_ref.at[pl.ds(first, count), :, column(c)]
        return pltpu.make_async_copy(source, query.at[c], arrive.at[c])

    def outward(c):
        target = out_ref.at[pl.ds(first, count), :, column(c)]
        return pltpu.make_async_copy(gated.at[c], target, leave.at[c])

    for c in range(ch):
        inward(c).start()
    for c in range(ch):
        inward(c).wait()
        for home in range(half):

            @pl.when(lax.rem(place_ref[0], half) == home)
            def _(c=c, home=home):
                for n in range(count):
                    for part in range(half):
                        lanes = slice(part * width, (part + 1) * width)
                        value = query[c, n, :, lanes].astype(jnp.float32) * pieces[home ^ part][c, n].astype(jnp.float32)
                        gated[c, n, :, lanes] = value.astype(jnp.bfloat16)

        outward(c).start()
    for c in range(ch):
        outward(c).wait()


def half_gate(place, queries, pieces, first, far):
    half, (ch, count, rows, width) = len(pieces), pieces[0].shape
    held = pltpu.VMEM((ch, count, rows, half * width), jnp.bfloat16)
    return pl.pallas_call(
        functools.partial(half_gate_kernel, first=first, half=half, far=far),
        in_specs=[pl.BlockSpec(memory_space=pltpu.SMEM), pl.BlockSpec(memory_space=pl.ANY)]
        + [pl.BlockSpec(memory_space=pltpu.VMEM)] * half,
        out_specs=pl.BlockSpec(memory_space=pl.ANY),
        out_shape=jax.ShapeDtypeStruct(queries.shape, jnp.bfloat16),
        scratch_shapes=[held, held, pltpu.SemaphoreType.DMA((ch,)), pltpu.SemaphoreType.DMA((ch,))],
        input_output_aliases={1: 0},
        compiler_params=params(8),
        cost_estimate=pl.CostEstimate(
            flops=half * pieces[0].size, bytes_accessed=6 * half * pieces[0].size, transcendentals=0
        ),
        name="half_gate",
    )(place, queries, *pieces)


def swap(pieces):
    count = lax.axis_size("seq")
    return [
        lax.ppermute(piece, "seq", [(source, source ^ step) for source in range(count)]) if step else piece
        for step, piece in enumerate(pieces)
    ]


def spread(whole):
    return lax.all_to_all(whole, "ch", split_axis=0, concat_axis=0, tiled=True)


def vacant_kernel(*refs):
    pass


def vacant(*arrays):
    return pl.pallas_call(
        vacant_kernel,
        out_specs=[pl.BlockSpec(memory_space=pl.ANY)] * len(arrays),
        out_shape=[jax.ShapeDtypeStruct(array.shape, array.dtype) for array in arrays],
        name="vacant",
    )()


def staged(times, place, step, *arrays):
    def round_of(_, held):
        return held[0] + 1, *step(held[0], *held[1:])

    return lax.fori_loop(0, times, round_of, (place, *arrays))[1:]


def shards(proj, short_w, long_filter):
    seq, ch = lax.axis_size("seq"), lax.axis_size("ch")
    tap_count, (seq_count, rows) = short_w.shape[0], proj.shape[:2]
    length, groups = long_filter.shape[1], long_filter.shape[0] // seq
    half = seq_count // 2
    place = lax.axis_index("seq").astype(jnp.int32).reshape(1)
    once = jnp.minimum(lax.axis_index("seq") + 1, 1)
    rim = from_behind(proj[:, rows - (tap_count - 1) :], ("seq", "ch"), 1).transpose(0, 2, 1, 3)
    taps = lax.all_gather(short_w, "ch", axis=2, tiled=True)
    turned = proj.transpose(0, 2, 1, 3)
    own = lax.dynamic_slice_in_dim(long_filter, place[0] * groups, groups, 0)
    filters = own.astype(jnp.float32).reshape(groups, 1, length)

    first = products(place, turned, rim, taps, 0, half, seq, ch, False)
    begun = first[0]

    def second_out(place, *held):
        (second,) = products(place, turned, rim, taps, half, half, seq, ch, True, after=[begun, place])
        queries = short_queries(turned, rim, taps, ch, after=[place])
        return queries, *split(spread(second))

    shape = jax.ShapeDtypeStruct((seq_count, rows, proj.shape[3]), proj.dtype)
    queries, *second = staged(once, place, second_out, *vacant(shape, *first))
    second_sent = second[0]

    def first_turn(place, *first):
        return long_conv(place, [spread(join(first, after=[place, second_sent]))], filters, seq)

    first = staged(once, place, first_turn, *swap(first))
    first_sent = first[0]

    def second_turn(place, *second):
        (second,) = long_conv(place, second, filters, seq, after=[first_sent])
        return split(spread(second))

    second = staged(once, place, second_turn, *swap(second))
    second_back = second[0]

    def first_gate(place, queries, *first):
        return gate(place, queries, [spread(join(first, after=[place, second_back]))], 0, seq), *first

    out = staged(once, place, first_gate, queries, *swap(first))[0]
    second = swap(second)
    out = half_gate(place, out, second[: seq // 2], half, False)
    return half_gate(place, out, second[seq // 2 :], half, True)


def solution(mesh):
    in_specs = (P(None, ("seq", "ch"), None, None), P(None, None, "ch"), P("ch", None))
    out_specs = P(None, ("seq", "ch"), None)
    return jax.shard_map(shards, mesh=mesh, in_specs=in_specs, out_specs=out_specs, check_vma=False)
```

```python
import functools
import math

import jax
import jax.numpy as jnp
from jax import lax
from jax.experimental import pallas as pl
from jax.experimental.pallas import tpu as pltpu
from jax.sharding import PartitionSpec as P

GSIZE = 16
MIB = 1024 * 1024


def from_behind(value, axis, steps):
    count = lax.axis_size(axis)
    first, last = (max(0, -steps), min(count, count - steps))
    return lax.ppermute(value, axis, [(source, source + steps) for source in range(first, last)])


def params(mib, *semantics):
    return pltpu.CompilerParams(dimension_semantics=semantics, vmem_limit_bytes=mib * MIB)


def filtered_rows(shifted, rows, rim, taps):
    count, reach = rows.shape[0], rim.shape[0]
    rows = rows.astype(jnp.float32)
    shifted[8 : 8 + count] = rows
    shifted[8 - reach : 8] = rim.astype(jnp.float32)
    total = taps[0:1] * rows
    for offset in range(1, reach + 1):
        total = total + taps[offset : offset + 1] * shifted[8 - offset : 8 - offset + count]
    return total


def product_kernel(place_ref, *refs, seq, outs):
    if outs == 1:
        product_body(place_ref[0], *refs, seq=seq, outs=outs)
        return
    for home in range(seq):
        pl.when(place_ref[0] == home)(functools.partial(product_body, home, *refs, seq=seq, outs=outs))


def product_body(place, key_ref, value_ref, key_rim, value_rim, taps_ref, *refs, seq, outs):
    shifted, outs = refs[-1], refs[-1 - outs : -1]
    count, width = key_ref.shape[0], outs[0].shape[-1]
    spans, lane = key_ref.shape[-1] // (seq * width), shifted.shape[-1]
    for span in range(spans):
        for part in range(seq):
            for low in range(0, width, lane):
                start = (span * seq + part) * width + low
                lanes = slice(start, start + lane)
                key_taps, value_taps = taps_ref[:, 1, lanes], taps_ref[:, 2, lanes]
                for n in range(count):
                    keys = filtered_rows(shifted.at[2 * n], key_ref[n, 0, :, lanes], key_rim[n, 0, :, lanes], key_taps)
                    values = filtered_rows(
                        shifted.at[2 * n + 1], value_ref[n, 0, :, lanes], value_rim[n, 0, :, lanes], value_taps
                    )
                    product = (keys * values).astype(jnp.bfloat16)
                    if len(outs) == 1:
                        outs[0][span, place ^ part, n, :, low : low + lane] = product
                    else:
                        outs[place ^ part][span, n, :, low : low + lane] = product


def products(place, proj, rim, taps, first, count, seq, ch, joined, after=()):
    rows, channels = proj.shape[2:]
    width = channels // (ch * seq)
    spans = math.gcd(ch, 8)
    block = spans * seq * width

    def of(component, depth):
        return pl.BlockSpec((1, 1, depth, block), lambda n, j, *_: (first + n, component, 0, j))

    if joined:
        out_specs = [pl.BlockSpec((spans, seq, 1, rows, width), lambda n, j, *_: (j, 0, n, 0, 0))]
        out_shape = [jax.ShapeDtypeStruct((ch, seq, count, rows, width), jnp.bfloat16)]
    else:
        out_specs = [pl.BlockSpec((spans, 1, rows, width), lambda n, j, *_: (j, n, 0, 0))] * seq
        out_shape = [jax.ShapeDtypeStruct((ch, count, rows, width), jnp.bfloat16)] * seq
    return pl.pallas_call(
        functools.partial(product_kernel, seq=seq, outs=len(out_shape)),
        grid_spec=pltpu.PrefetchScalarGridSpec(
            num_scalar_prefetch=1,
            grid=(count, ch // spans),
            in_specs=[of(1, rows), of(2, rows), of(1, rim.shape[2]), of(2, rim.shape[2])]
            + [pl.BlockSpec(taps.shape[:2] + (block,), lambda n, j, *_: (0, 0, j))]
            + [pl.BlockSpec(memory_space=pl.ANY)] * len(after),
            out_specs=out_specs,
            scratch_shapes=[pltpu.VMEM((2 * count, rows + 8, math.gcd(width, 128)), jnp.float32)],
        ),
        out_shape=out_shape,
        compiler_params=params(14, "arbitrary", "arbitrary"),
        cost_estimate=pl.CostEstimate(
            flops=20 * count * rows * channels, bytes_accessed=6 * count * rows * channels, transcendentals=0
        ),
        name="products",
    )(place, proj, proj, rim, rim, taps, *after)


def queries_kernel(query_ref, query_rim, query_taps, *refs):
    out_ref, shifted = refs[-2:]
    lane = shifted.shape[-1]
    for low in range(0, query_ref.shape[-1], lane):
        lanes = slice(low, low + lane)
        taps = query_taps[:, 0, lanes]
        for n in range(query_ref.shape[0]):
            total = filtered_rows(shifted.at[n], query_ref[n, 0, :, lanes], query_rim[n, 0, :, lanes], taps)
            out_ref[n, :, lanes] = total.astype(jnp.bfloat16)


def short_queries(proj, rim, taps, ch, after=()):
    count, _, rows, channels = proj.shape
    block = channels // ch * math.gcd(ch, 2)

    def of(depth):
        return pl.BlockSpec((count, 1, depth, block), lambda j: (0, 0, 0, j))

    return pl.pallas_call(
        queries_kernel,
        grid=(channels // block,),
        in_specs=[of(rows), of(rim.shape[2]), pl.BlockSpec(taps.shape[:2] + (block,), lambda j: (0, 0, j))]
        + [pl.BlockSpec(memory_space=pl.ANY)] * len(after),
        out_specs=pl.BlockSpec((count, rows, block), lambda j: (0, 0, j)),
        out_shape=jax.ShapeDtypeStruct((count, rows, channels), jnp.bfloat16),
        scratch_shapes=[pltpu.VMEM((count, rows + 8, math.gcd(block, 128)), jnp.float32)],
        compiler_params=params(8, "arbitrary"),
        cost_estimate=pl.CostEstimate(
            flops=8 * count * rows * channels, bytes_accessed=4 * count * rows * channels, transcendentals=0
        ),
        name="queries",
    )(proj, rim, taps, *after)


def build_table(filter_row, table_ref):
    tile, length = table_ref.shape
    skewed = pltpu.roll(jnp.broadcast_to(filter_row, (tile, length)), 0, 1, stride=1, stride_axis=0)
    source = lax.broadcasted_iota(jnp.int32, (tile, tile), 0)
    target = lax.broadcasted_iota(jnp.int32, (tile, tile), 1)
    table_ref[:, :tile] = jnp.where(target >= source, skewed[:, :tile], 0.0).astype(jnp.bfloat16)
    if length > tile:
        table_ref[:, tile:] = skewed[:, tile:].astype(jnp.bfloat16)


def convolve(filter_ref, turned, table, acc, done, count):
    tile, length = table.shape[1:]
    tiles, strip = length // tile, count * GSIZE
    for group in range(table.shape[0]):
        build_table(filter_ref[group], table.at[group])
    for group in range(table.shape[0]):
        own = slice(group * GSIZE, (group + 1) * GSIZE)
        mine = turned[:, own, :].reshape(tiles * strip, tile)
        for lag in range(tiles):
            part = jnp.dot(
                mine[: (tiles - lag) * strip],
                table[group, :, lag * tile : (lag + 1) * tile],
                preferred_element_type=jnp.float32,
            )
            if lag == 0:
                acc[group] = part
            else:
                acc[group, lag * strip :] += part
        done[:, own, :] = acc[group].astype(jnp.bfloat16).reshape(tiles * count, GSIZE, tile)


def pieces_of(tile_index, span, ch):
    first, last, found = tile_index * span, (tile_index + 1) * span, []
    while first < last:
        stop = min(last, (first // ch + 1) * ch)
        found.append((first // ch, first % ch, first % ch + stop - first))
        first = stop
    return found


def conv_kernel(place_ref, *refs, seq, joined):
    turned, table, acc, done, gathered = refs[-5:]
    ch, _, count, rows, width = gathered.shape
    outs = refs[-5 - seq : -5] if joined else refs[-6:-5]
    ins, filter_ref = (refs[:1], refs[1]) if joined else (refs[:seq], refs[seq])
    tile, length = table.shape[1:]
    tiles, span = length // tile, tile // rows
    if joined:
        source = ins[0]
    else:
        source = gathered
        for step in range(seq):
            gathered[:, step] = ins[step][...]
    for u in range(tiles):
        for n in range(count):
            blocks = [
                source[low:high, place_ref[0] ^ z, n].reshape((high - low) * rows, width)
                for z, low, high in pieces_of(u, span, ch)
            ]
            block = blocks[0] if len(blocks) == 1 else jnp.concatenate(blocks, axis=0)
            turned[u * count + n] = block.T
    convolve(filter_ref, turned, table, acc, done, count)
    target = gathered if joined else outs[0]
    for u in range(tiles):
        for n in range(count):
            block, start = done[u * count + n].T, 0
            for z, low, high in pieces_of(u, span, ch):
                stop = start + (high - low) * rows
                target[low:high, place_ref[0] ^ z, n] = block[start:stop].reshape(high - low, rows, width)
                start = stop
    if joined:
        for step in range(seq):
            outs[step][...] = gathered[:, step]


def conv_scratch(count, width, tile, length):
    tiles, groups = length // tile, width // GSIZE
    return [
        pltpu.VMEM((tiles * count, width, tile), jnp.bfloat16),
        pltpu.VMEM((groups, tile, length), jnp.bfloat16),
        pltpu.VMEM((groups, tiles * count * GSIZE, tile), jnp.float32),
        pltpu.VMEM((tiles * count, width, tile), jnp.bfloat16),
    ]


def long_conv(place, pieces, filters, seq, after=()):
    joined = len(pieces) == 1
    ch, (count, rows, channels) = pieces[0].shape[0], pieces[0].shape[-3:]
    groups, _, length = filters.shape
    width, tile = math.gcd(channels, 128), min(256, length)
    tiles = length // tile
    one = pl.BlockSpec((ch, seq, count, rows, width), lambda j, place: (0, 0, 0, 0, j))
    part = pl.BlockSpec((ch, count, rows, width), lambda j, place: (0, 0, 0, j))
    whole_shape = jax.ShapeDtypeStruct((ch, seq, count, rows, channels), jnp.bfloat16)
    part_shape = jax.ShapeDtypeStruct((ch, count, rows, channels), jnp.bfloat16)
    return pl.pallas_call(
        functools.partial(conv_kernel, seq=seq, joined=joined),
        grid_spec=pltpu.PrefetchScalarGridSpec(
            num_scalar_prefetch=1,
            grid=(channels // width,),
            in_specs=([one] if joined else [part] * seq)
            + [pl.BlockSpec((width // GSIZE, 1, length), lambda j, place: (j, 0, 0))]
            + [pl.BlockSpec(memory_space=pl.ANY)] * len(after),
            out_specs=[part] * seq if joined else [one],
            scratch_shapes=conv_scratch(count, width, tile, length)
            + [pltpu.VMEM((ch, seq, count, rows, width), jnp.bfloat16)],
        ),
        out_shape=[part_shape] * seq if joined else [whole_shape],
        compiler_params=params(32, "arbitrary"),
        cost_estimate=pl.CostEstimate(
            flops=groups * (tiles + 1) * tiles * tile * tile * count * GSIZE,
            bytes_accessed=4 * ch * seq * count * rows * channels,
            transcendentals=0,
        ),
        name="long_conv",
    )(place, *pieces, filters, *after)


def join_kernel(*refs, seq):
    for step in range(seq):
        refs[-1][:, step] = refs[step][...]


def join(pieces, after=()):
    seq, (ch, count, rows, width) = len(pieces), pieces[0].shape
    spans = math.gcd(ch, 4)
    return pl.pallas_call(
        functools.partial(join_kernel, seq=seq),
        grid=(ch // spans,),
        in_specs=[pl.BlockSpec((spans, count, rows, width), lambda j: (j, 0, 0, 0))] * seq
        + [pl.BlockSpec(memory_space=pl.ANY)] * len(after),
        out_specs=pl.BlockSpec((spans, seq, count, rows, width), lambda j: (j, 0, 0, 0, 0)),
        out_shape=jax.ShapeDtypeStruct((ch, seq, count, rows, width), jnp.bfloat16),
        compiler_params=params(8, "arbitrary"),
        cost_estimate=pl.CostEstimate(flops=0, bytes_accessed=4 * seq * pieces[0].size, transcendentals=0),
        name="join",
    )(*pieces, *after)


def split_kernel(whole_ref, *refs, seq):
    for step in range(seq):
        refs[step - seq][...] = whole_ref[:, step]


def split(whole, after=()):
    ch, seq, count, rows, width = whole.shape
    spans = math.gcd(ch, 4)
    return pl.pallas_call(
        functools.partial(split_kernel, seq=seq),
        grid=(ch // spans,),
        in_specs=[pl.BlockSpec((spans, seq, count, rows, width), lambda j: (j, 0, 0, 0, 0))]
        + [pl.BlockSpec(memory_space=pl.ANY)] * len(after),
        out_specs=[pl.BlockSpec((spans, count, rows, width), lambda j: (j, 0, 0, 0))] * seq,
        out_shape=[jax.ShapeDtypeStruct((ch, count, rows, width), jnp.bfloat16)] * seq,
        compiler_params=params(8, "arbitrary"),
        cost_estimate=pl.CostEstimate(flops=0, bytes_accessed=4 * whole.size, transcendentals=0),
        name="split",
    )(whole, *after)


def gate_kernel(place_ref, query_ref, *refs, seq, joined):
    out_ref = refs[-1]
    rows, width = out_ref.shape[1], refs[0].shape[-1]
    for home in range(1 if joined else seq):

        def gated(home=home):
            for n in range(query_ref.shape[0]):
                for span in range(refs[0].shape[0]):
                    for part in range(seq):
                        start = (span * seq + part) * width
                        lanes = slice(start, start + width)
                        if joined:
                            filtered = refs[0][span, place_ref[0] ^ part, n]
                        else:
                            filtered = refs[home ^ part][span, n]
                        value = query_ref[n, :, lanes].astype(jnp.float32) * filtered.astype(jnp.float32)
                        out_ref[n, :, lanes] = value.astype(jnp.bfloat16)

        if joined:
            gated()
        else:
            pl.when(place_ref[0] == home)(gated)


def gate(place, queries, pieces, first, seq):
    joined = len(pieces) == 1
    ch, (count, rows, width) = pieces[0].shape[0], pieces[0].shape[-3:]
    spans, start = math.gcd(ch, 2), first // count
    spec = pl.BlockSpec((count, rows, spans * seq * width), lambda j, place: (start, 0, j))
    one = pl.BlockSpec((spans, seq, count, rows, width), lambda j, place: (j, 0, 0, 0, 0))
    part = pl.BlockSpec((spans, count, rows, width), lambda j, place: (j, 0, 0, 0))
    return pl.pallas_call(
        functools.partial(gate_kernel, seq=seq, joined=joined),
        grid_spec=pltpu.PrefetchScalarGridSpec(
            num_scalar_prefetch=1,
            grid=(ch // spans,),
            in_specs=[spec] + ([one] if joined else [part] * seq),
            out_specs=spec,
        ),
        out_shape=jax.ShapeDtypeStruct(queries.shape, jnp.bfloat16),
        input_output_aliases={1: 0},
        compiler_params=params(8, "arbitrary"),
        cost_estimate=pl.CostEstimate(
            flops=count * rows * queries.shape[-1],
            bytes_accessed=6 * count * rows * queries.shape[-1],
            transcendentals=0,
        ),
        name="gate",
    )(place, queries, *pieces)


def half_gate_kernel(place_ref, queries_ref, *refs, first, half, far):
    pieces, out_ref, query, gated, arrive, leave = refs[:half], *refs[-5:]
    ch, count, _, width = pieces[0].shape
    block = half * width

    def column(c):
        place = c * 2 + (lax.div(place_ref[0], half) ^ int(far))
        return pl.ds(pl.multiple_of(place * block, block), block)

    def inward(c):
        source = queries_ref.at[pl.ds(first, count), :, column(c)]
        return pltpu.make_async_copy(source, query.at[c], arrive.at[c])

    def outward(c):
        target = out_ref.at[pl.ds(first, count), :, column(c)]
        return pltpu.make_async_copy(gated.at[c], target, leave.at[c])

    for c in range(ch):
        inward(c).start()
    for c in range(ch):
        inward(c).wait()
        for home in range(half):

            @pl.when(lax.rem(place_ref[0], half) == home)
            def _(c=c, home=home):
                for n in range(count):
                    for part in range(half):
                        lanes = slice(part * width, (part + 1) * width)
                        value = query[c, n, :, lanes].astype(jnp.float32) * pieces[home ^ part][c, n].astype(jnp.float32)
                        gated[c, n, :, lanes] = value.astype(jnp.bfloat16)

        outward(c).start()
    for c in range(ch):
        outward(c).wait()


def half_gate(place, queries, pieces, first, far):
    half, (ch, count, rows, width) = len(pieces), pieces[0].shape
    held = pltpu.VMEM((ch, count, rows, half * width), jnp.bfloat16)
    return pl.pallas_call(
        functools.partial(half_gate_kernel, first=first, half=half, far=far),
        in_specs=[pl.BlockSpec(memory_space=pltpu.SMEM), pl.BlockSpec(memory_space=pl.ANY)]
        + [pl.BlockSpec(memory_space=pltpu.VMEM)] * half,
        out_specs=pl.BlockSpec(memory_space=pl.ANY),
        out_shape=jax.ShapeDtypeStruct(queries.shape, jnp.bfloat16),
        scratch_shapes=[held, held, pltpu.SemaphoreType.DMA((ch,)), pltpu.SemaphoreType.DMA((ch,))],
        input_output_aliases={1: 0},
        compiler_params=params(8),
        cost_estimate=pl.CostEstimate(
            flops=half * pieces[0].size, bytes_accessed=6 * half * pieces[0].size, transcendentals=0
        ),
        name="half_gate",
    )(place, queries, *pieces)


def step_gate_kernel(place_ref, queries_ref, piece_ref, *refs, first, step, seq):
    out_ref, query, gated, arrive, leave = refs
    ch, count, _, width = piece_ref.shape

    def column(c):
        return pl.ds(pl.multiple_of((c * seq + (place_ref[0] ^ step)) * width, width), width)

    def inward(c):
        source = queries_ref.at[pl.ds(first, count), :, column(c)]
        return pltpu.make_async_copy(source, query.at[c], arrive.at[c])

    def outward(c):
        target = out_ref.at[pl.ds(first, count), :, column(c)]
        return pltpu.make_async_copy(gated.at[c], target, leave.at[c])

    for c in range(ch):
        inward(c).start()
    for c in range(ch):
        inward(c).wait()
        gated[c] = (query[c].astype(jnp.float32) * piece_ref[c].astype(jnp.float32)).astype(jnp.bfloat16)
        outward(c).start()
    for c in range(ch):
        outward(c).wait()


def step_gate(place, queries, piece, first, step, seq):
    held = pltpu.VMEM(piece.shape, jnp.bfloat16)
    semaphores = pltpu.SemaphoreType.DMA(piece.shape[:1])
    return pl.pallas_call(
        functools.partial(step_gate_kernel, first=first, step=step, seq=seq),
        in_specs=[
            pl.BlockSpec(memory_space=pltpu.SMEM),
            pl.BlockSpec(memory_space=pl.ANY),
            pl.BlockSpec(memory_space=pltpu.VMEM),
        ],
        out_specs=pl.BlockSpec(memory_space=pl.ANY),
        out_shape=jax.ShapeDtypeStruct(queries.shape, jnp.bfloat16),
        scratch_shapes=[held, held, semaphores, semaphores],
        input_output_aliases={1: 0},
        compiler_params=params(8),
        cost_estimate=pl.CostEstimate(flops=piece.size, bytes_accessed=6 * piece.size, transcendentals=0),
        name="step_gate",
    )(place, queries, piece)


def swap(pieces):
    count = lax.axis_size("seq")
    return [
        lax.ppermute(piece, "seq", [(source, source ^ step) for source in range(count)]) if step else piece
        for step, piece in enumerate(pieces)
    ]


def spread(whole):
    return lax.all_to_all(whole, "ch", split_axis=0, concat_axis=0, tiled=True)


def vacant_kernel(*refs):
    pass


def vacant(*arrays):
    return pl.pallas_call(
        vacant_kernel,
        out_specs=[pl.BlockSpec(memory_space=pl.ANY)] * len(arrays),
        out_shape=[jax.ShapeDtypeStruct(array.shape, array.dtype) for array in arrays],
        name="vacant",
    )()


def staged(times, place, step, *arrays):
    def round_of(_, held):
        return held[0] + 1, *step(held[0], *held[1:])

    return lax.fori_loop(0, times, round_of, (place, *arrays))[1:]


def shards(proj, short_w, long_filter):
    seq, ch = lax.axis_size("seq"), lax.axis_size("ch")
    tap_count, (seq_count, rows) = short_w.shape[0], proj.shape[:2]
    length, groups = long_filter.shape[1], long_filter.shape[0] // seq
    half = seq_count // 2
    place = lax.axis_index("seq").astype(jnp.int32).reshape(1)
    once = jnp.minimum(lax.axis_index("seq") + 1, 1)
    rim = from_behind(proj[:, rows - (tap_count - 1) :], ("seq", "ch"), 1).transpose(0, 2, 1, 3)
    taps = lax.all_gather(short_w, "ch", axis=2, tiled=True)
    turned = proj.transpose(0, 2, 1, 3)
    own = lax.dynamic_slice_in_dim(long_filter, place[0] * groups, groups, 0)
    filters = own.astype(jnp.float32).reshape(groups, 1, length)

    first = products(place, turned, rim, taps, 0, half, seq, ch, False)
    begun = first[0]

    def second_out(place, *held):
        (second,) = products(place, turned, rim, taps, half, half, seq, ch, True, after=[begun, place])
        queries = short_queries(turned, rim, taps, ch, after=[place])
        return queries, *split(spread(second))

    shape = jax.ShapeDtypeStruct((seq_count, rows, proj.shape[3]), proj.dtype)
    queries, *second = staged(once, place, second_out, *vacant(shape, *first))
    second_sent = second[0]

    def first_turn(place, *first):
        whole = spread(join(first[::-1], after=[place, second_sent]))
        return long_conv(place, [whole], filters, seq)[::-1]

    first = staged(once, place, first_turn, *swap(first)[::-1])[::-1]
    first_sent = first[0]

    def second_turn(place, *second):
        (second,) = long_conv(place, second, filters, seq, after=[first_sent])
        return split(spread(second))

    second = staged(once, place, second_turn, *swap(second))
    second_back = second[0]

    def first_gate(place, queries, *first):
        return gate(place, queries, [spread(join(first, after=[place, second_back]))], 0, seq), *first

    out = staged(once, place, first_gate, queries, *swap(first))[0]
    second = swap(second)
    out = half_gate(place, out, second[: seq // 2], half, False)
    if second[0].shape[-1] % 128:
        return half_gate(place, out, second[seq // 2 :], half, True)
    for step in range(seq // 2, seq):
        out = step_gate(place, out, second[step], half, step, seq)
    return out


def solution(mesh):
    in_specs = (P(None, ("seq", "ch"), None, None), P(None, None, "ch"), P("ch", None))
    out_specs = P(None, ("seq", "ch"), None)
    return jax.shard_map(shards, mesh=mesh, in_specs=in_specs, out_specs=out_specs, check_vma=False)
```

```python
import functools
import math

import jax
import jax.numpy as jnp
from jax import lax
from jax.experimental import pallas as pl
from jax.experimental.pallas import tpu as pltpu
from jax.sharding import PartitionSpec as P

GSIZE = 16
MIB = 1024 * 1024


def from_behind(value, axis, steps):
    count = lax.axis_size(axis)
    first, last = (max(0, -steps), min(count, count - steps))
    return lax.ppermute(value, axis, [(source, source + steps) for source in range(first, last)])


def params(mib, *semantics):
    return pltpu.CompilerParams(dimension_semantics=semantics, vmem_limit_bytes=mib * MIB)


def filtered_rows(shifted, rows, rim, taps):
    count, reach = rows.shape[0], rim.shape[0]
    rows = rows.astype(jnp.float32)
    shifted[8 : 8 + count] = rows
    shifted[8 - reach : 8] = rim.astype(jnp.float32)
    total = taps[0:1] * rows
    for offset in range(1, reach + 1):
        total = total + taps[offset : offset + 1] * shifted[8 - offset : 8 - offset + count]
    return total


def product_kernel(place_ref, *refs, seq, steps):
    if steps is None:
        product_body(place_ref[0], *refs, seq=seq, steps=steps)
        return
    for home in range(seq):
        pl.when(place_ref[0] == home)(functools.partial(product_body, home, *refs, seq=seq, steps=steps))


def product_body(place, key_ref, value_ref, key_rim, value_rim, taps_ref, *refs, seq, steps):
    shifted, outs = refs[-1], refs[-1 - (1 if steps is None else len(steps)) : -1]
    count, width = key_ref.shape[0], outs[0].shape[-1]
    spans, lane = key_ref.shape[-1] // (seq * width), shifted.shape[-1]
    for span in range(spans):
        for part in range(seq):
            if steps is not None and place ^ part not in steps:
                continue
            for low in range(0, width, lane):
                start = (span * seq + part) * width + low
                lanes = slice(start, start + lane)
                key_taps, value_taps = taps_ref[:, 1, lanes], taps_ref[:, 2, lanes]
                for n in range(count):
                    keys = filtered_rows(shifted.at[2 * n], key_ref[n, 0, :, lanes], key_rim[n, 0, :, lanes], key_taps)
                    values = filtered_rows(
                        shifted.at[2 * n + 1], value_ref[n, 0, :, lanes], value_rim[n, 0, :, lanes], value_taps
                    )
                    product = (keys * values).astype(jnp.bfloat16)
                    if steps is None:
                        outs[0][span, place ^ part, n, :, low : low + lane] = product
                    else:
                        outs[steps.index(place ^ part)][span, n, :, low : low + lane] = product


def products(place, proj, rim, taps, first, count, seq, ch, steps=None, after=()):
    rows, channels = proj.shape[2:]
    width = channels // (ch * seq)
    spans = math.gcd(ch, 8)
    block = spans * seq * width

    def of(component, depth):
        return pl.BlockSpec((1, 1, depth, block), lambda n, j, *_: (first + n, component, 0, j))

    if steps is None:
        out_specs = [pl.BlockSpec((spans, seq, 1, rows, width), lambda n, j, *_: (j, 0, n, 0, 0))]
        out_shape = [jax.ShapeDtypeStruct((ch, seq, count, rows, width), jnp.bfloat16)]
    else:
        out_specs = [pl.BlockSpec((spans, 1, rows, width), lambda n, j, *_: (j, n, 0, 0))] * len(steps)
        out_shape = [jax.ShapeDtypeStruct((ch, count, rows, width), jnp.bfloat16)] * len(steps)
    return pl.pallas_call(
        functools.partial(product_kernel, seq=seq, steps=steps),
        grid_spec=pltpu.PrefetchScalarGridSpec(
            num_scalar_prefetch=1,
            grid=(count, ch // spans),
            in_specs=[of(1, rows), of(2, rows), of(1, rim.shape[2]), of(2, rim.shape[2])]
            + [pl.BlockSpec(taps.shape[:2] + (block,), lambda n, j, *_: (0, 0, j))]
            + [pl.BlockSpec(memory_space=pl.ANY)] * len(after),
            out_specs=out_specs,
            scratch_shapes=[pltpu.VMEM((2 * count, rows + 8, math.gcd(width, 128)), jnp.float32)],
        ),
        out_shape=out_shape,
        compiler_params=params(14, "arbitrary", "arbitrary"),
        cost_estimate=pl.CostEstimate(
            flops=20 * count * rows * channels, bytes_accessed=6 * count * rows * channels, transcendentals=0
        ),
        name="products",
    )(place, proj, proj, rim, rim, taps, *after)


def queries_kernel(query_ref, query_rim, query_taps, *refs):
    out_ref, shifted = refs[-2:]
    lane = shifted.shape[-1]
    for low in range(0, query_ref.shape[-1], lane):
        lanes = slice(low, low + lane)
        taps = query_taps[:, 0, lanes]
        for n in range(query_ref.shape[0]):
            total = filtered_rows(shifted.at[n], query_ref[n, 0, :, lanes], query_rim[n, 0, :, lanes], taps)
            out_ref[n, :, lanes] = total.astype(jnp.bfloat16)


def short_queries(proj, rim, taps, ch, after=()):
    count, _, rows, channels = proj.shape
    block = channels // ch * math.gcd(ch, 2)

    def of(depth):
        return pl.BlockSpec((count, 1, depth, block), lambda j: (0, 0, 0, j))

    return pl.pallas_call(
        queries_kernel,
        grid=(channels // block,),
        in_specs=[of(rows), of(rim.shape[2]), pl.BlockSpec(taps.shape[:2] + (block,), lambda j: (0, 0, j))]
        + [pl.BlockSpec(memory_space=pl.ANY)] * len(after),
        out_specs=pl.BlockSpec((count, rows, block), lambda j: (0, 0, j)),
        out_shape=jax.ShapeDtypeStruct((count, rows, channels), jnp.bfloat16),
        scratch_shapes=[pltpu.VMEM((count, rows + 8, math.gcd(block, 128)), jnp.float32)],
        compiler_params=params(8, "arbitrary"),
        cost_estimate=pl.CostEstimate(
            flops=8 * count * rows * channels, bytes_accessed=4 * count * rows * channels, transcendentals=0
        ),
        name="queries",
    )(proj, rim, taps, *after)


def build_table(filter_row, table_ref):
    tile, length = table_ref.shape
    skewed = pltpu.roll(jnp.broadcast_to(filter_row, (tile, length)), 0, 1, stride=1, stride_axis=0)
    source = lax.broadcasted_iota(jnp.int32, (tile, tile), 0)
    target = lax.broadcasted_iota(jnp.int32, (tile, tile), 1)
    table_ref[:, :tile] = jnp.where(target >= source, skewed[:, :tile], 0.0).astype(jnp.bfloat16)
    if length > tile:
        table_ref[:, tile:] = skewed[:, tile:].astype(jnp.bfloat16)


def convolve(filter_ref, turned, table, acc, done, count):
    tile, length = table.shape[1:]
    tiles, strip = length // tile, count * GSIZE
    for group in range(table.shape[0]):
        build_table(filter_ref[group], table.at[group])
    for group in range(table.shape[0]):
        own = slice(group * GSIZE, (group + 1) * GSIZE)
        mine = turned[:, own, :].reshape(tiles * strip, tile)
        for lag in range(tiles):
            part = jnp.dot(
                mine[: (tiles - lag) * strip],
                table[group, :, lag * tile : (lag + 1) * tile],
                preferred_element_type=jnp.float32,
            )
            if lag == 0:
                acc[group] = part
            else:
                acc[group, lag * strip :] += part
        done[:, own, :] = acc[group].astype(jnp.bfloat16).reshape(tiles * count, GSIZE, tile)


def pieces_of(tile_index, span, ch):
    first, last, found = tile_index * span, (tile_index + 1) * span, []
    while first < last:
        stop = min(last, (first // ch + 1) * ch)
        found.append((first // ch, first % ch, first % ch + stop - first))
        first = stop
    return found


def conv_kernel(place_ref, *refs, seq, joined):
    turned, table, acc, done, gathered = refs[-5:]
    ch, _, count, rows, width = gathered.shape
    outs = refs[-5 - seq : -5] if joined else refs[-6:-5]
    ins, filter_ref = (refs[:1], refs[1]) if joined else (refs[:seq], refs[seq])
    tile, length = table.shape[1:]
    tiles, span = length // tile, tile // rows
    if joined:
        source = ins[0]
    else:
        source = gathered
        for step in range(seq):
            gathered[:, step] = ins[step][...]
    for u in range(tiles):
        for n in range(count):
            blocks = [
                source[low:high, place_ref[0] ^ z, n].reshape((high - low) * rows, width)
                for z, low, high in pieces_of(u, span, ch)
            ]
            block = blocks[0] if len(blocks) == 1 else jnp.concatenate(blocks, axis=0)
            turned[u * count + n] = block.T
    convolve(filter_ref, turned, table, acc, done, count)
    target = gathered if joined else outs[0]
    for u in range(tiles):
        for n in range(count):
            block, start = done[u * count + n].T, 0
            for z, low, high in pieces_of(u, span, ch):
                stop = start + (high - low) * rows
                target[low:high, place_ref[0] ^ z, n] = block[start:stop].reshape(high - low, rows, width)
                start = stop
    if joined:
        for step in range(seq):
            outs[step][...] = gathered[:, step]


def conv_scratch(count, width, tile, length):
    tiles, groups = length // tile, width // GSIZE
    return [
        pltpu.VMEM((tiles * count, width, tile), jnp.bfloat16),
        pltpu.VMEM((groups, tile, length), jnp.bfloat16),
        pltpu.VMEM((groups, tiles * count * GSIZE, tile), jnp.float32),
        pltpu.VMEM((tiles * count, width, tile), jnp.bfloat16),
    ]


def long_conv(place, pieces, filters, seq, after=()):
    joined = len(pieces) == 1
    ch, (count, rows, channels) = pieces[0].shape[0], pieces[0].shape[-3:]
    groups, _, length = filters.shape
    width, tile = math.gcd(channels, 128), min(256, length)
    tiles = length // tile
    one = pl.BlockSpec((ch, seq, count, rows, width), lambda j, place: (0, 0, 0, 0, j))
    part = pl.BlockSpec((ch, count, rows, width), lambda j, place: (0, 0, 0, j))
    whole_shape = jax.ShapeDtypeStruct((ch, seq, count, rows, channels), jnp.bfloat16)
    part_shape = jax.ShapeDtypeStruct((ch, count, rows, channels), jnp.bfloat16)
    return pl.pallas_call(
        functools.partial(conv_kernel, seq=seq, joined=joined),
        grid_spec=pltpu.PrefetchScalarGridSpec(
            num_scalar_prefetch=1,
            grid=(channels // width,),
            in_specs=([one] if joined else [part] * seq)
            + [pl.BlockSpec((width // GSIZE, 1, length), lambda j, place: (j, 0, 0))]
            + [pl.BlockSpec(memory_space=pl.ANY)] * len(after),
            out_specs=[part] * seq if joined else [one],
            scratch_shapes=conv_scratch(count, width, tile, length)
            + [pltpu.VMEM((ch, seq, count, rows, width), jnp.bfloat16)],
        ),
        out_shape=[part_shape] * seq if joined else [whole_shape],
        compiler_params=params(32, "arbitrary"),
        cost_estimate=pl.CostEstimate(
            flops=groups * (tiles + 1) * tiles * tile * tile * count * GSIZE,
            bytes_accessed=4 * ch * seq * count * rows * channels,
            transcendentals=0,
        ),
        name="long_conv",
    )(place, *pieces, filters, *after)


def join_kernel(*refs, seq):
    for step in range(seq):
        refs[-1][:, step] = refs[step][...]


def join(pieces, after=()):
    seq, (ch, count, rows, width) = len(pieces), pieces[0].shape
    spans = math.gcd(ch, 4)
    return pl.pallas_call(
        functools.partial(join_kernel, seq=seq),
        grid=(ch // spans,),
        in_specs=[pl.BlockSpec((spans, count, rows, width), lambda j: (j, 0, 0, 0))] * seq
        + [pl.BlockSpec(memory_space=pl.ANY)] * len(after),
        out_specs=pl.BlockSpec((spans, seq, count, rows, width), lambda j: (j, 0, 0, 0, 0)),
        out_shape=jax.ShapeDtypeStruct((ch, seq, count, rows, width), jnp.bfloat16),
        compiler_params=params(8, "arbitrary"),
        cost_estimate=pl.CostEstimate(flops=0, bytes_accessed=4 * seq * pieces[0].size, transcendentals=0),
        name="join",
    )(*pieces, *after)


def split_kernel(whole_ref, *refs, seq):
    for step in range(seq):
        refs[step - seq][...] = whole_ref[:, step]


def split(whole, after=()):
    ch, seq, count, rows, width = whole.shape
    spans = math.gcd(ch, 4)
    return pl.pallas_call(
        functools.partial(split_kernel, seq=seq),
        grid=(ch // spans,),
        in_specs=[pl.BlockSpec((spans, seq, count, rows, width), lambda j: (j, 0, 0, 0, 0))]
        + [pl.BlockSpec(memory_space=pl.ANY)] * len(after),
        out_specs=[pl.BlockSpec((spans, count, rows, width), lambda j: (j, 0, 0, 0))] * seq,
        out_shape=[jax.ShapeDtypeStruct((ch, count, rows, width), jnp.bfloat16)] * seq,
        compiler_params=params(8, "arbitrary"),
        cost_estimate=pl.CostEstimate(flops=0, bytes_accessed=4 * whole.size, transcendentals=0),
        name="split",
    )(whole, *after)


def gate_kernel(place_ref, query_ref, *refs, seq, joined):
    out_ref = refs[-1]
    rows, width = out_ref.shape[1], refs[0].shape[-1]
    for home in range(1 if joined else seq):

        def gated(home=home):
            for n in range(query_ref.shape[0]):
                for span in range(refs[0].shape[0]):
                    for part in range(seq):
                        start = (span * seq + part) * width
                        lanes = slice(start, start + width)
                        if joined:
                            filtered = refs[0][span, place_ref[0] ^ part, n]
                        else:
                            filtered = refs[home ^ part][span, n]
                        value = query_ref[n, :, lanes].astype(jnp.float32) * filtered.astype(jnp.float32)
                        out_ref[n, :, lanes] = value.astype(jnp.bfloat16)

        if joined:
            gated()
        else:
            pl.when(place_ref[0] == home)(gated)


def gate(place, queries, pieces, first, seq):
    joined = len(pieces) == 1
    ch, (count, rows, width) = pieces[0].shape[0], pieces[0].shape[-3:]
    spans, start = math.gcd(ch, 2), first // count
    spec = pl.BlockSpec((count, rows, spans * seq * width), lambda j, place: (start, 0, j))
    one = pl.BlockSpec((spans, seq, count, rows, width), lambda j, place: (j, 0, 0, 0, 0))
    part = pl.BlockSpec((spans, count, rows, width), lambda j, place: (j, 0, 0, 0))
    return pl.pallas_call(
        functools.partial(gate_kernel, seq=seq, joined=joined),
        grid_spec=pltpu.PrefetchScalarGridSpec(
            num_scalar_prefetch=1,
            grid=(ch // spans,),
            in_specs=[spec] + ([one] if joined else [part] * seq),
            out_specs=spec,
        ),
        out_shape=jax.ShapeDtypeStruct(queries.shape, jnp.bfloat16),
        input_output_aliases={1: 0},
        compiler_params=params(8, "arbitrary"),
        cost_estimate=pl.CostEstimate(
            flops=count * rows * queries.shape[-1],
            bytes_accessed=6 * count * rows * queries.shape[-1],
            transcendentals=0,
        ),
        name="gate",
    )(place, queries, *pieces)


def half_gate_kernel(place_ref, queries_ref, *refs, first, half, far):
    pieces, out_ref, query, gated, arrive, leave = refs[:half], *refs[-5:]
    ch, count, _, width = pieces[0].shape
    block = half * width

    def column(c):
        place = c * 2 + (lax.div(place_ref[0], half) ^ int(far))
        return pl.ds(pl.multiple_of(place * block, block), block)

    def inward(c):
        source = queries_ref.at[pl.ds(first, count), :, column(c)]
        return pltpu.make_async_copy(source, query.at[c], arrive.at[c])

    def outward(c):
        target = out_ref.at[pl.ds(first, count), :, column(c)]
        return pltpu.make_async_copy(gated.at[c], target, leave.at[c])

    for c in range(ch):
        inward(c).start()
    for c in range(ch):
        inward(c).wait()
        for home in range(half):

            @pl.when(lax.rem(place_ref[0], half) == home)
            def _(c=c, home=home):
                for n in range(count):
                    for part in range(half):
                        lanes = slice(part * width, (part + 1) * width)
                        value = query[c, n, :, lanes].astype(jnp.float32) * pieces[home ^ part][c, n].astype(jnp.float32)
                        gated[c, n, :, lanes] = value.astype(jnp.bfloat16)

        outward(c).start()
    for c in range(ch):
        outward(c).wait()


def half_gate(place, queries, pieces, first, far):
    half, (ch, count, rows, width) = len(pieces), pieces[0].shape
    held = pltpu.VMEM((ch, count, rows, half * width), jnp.bfloat16)
    return pl.pallas_call(
        functools.partial(half_gate_kernel, first=first, half=half, far=far),
        in_specs=[pl.BlockSpec(memory_space=pltpu.SMEM), pl.BlockSpec(memory_space=pl.ANY)]
        + [pl.BlockSpec(memory_space=pltpu.VMEM)] * half,
        out_specs=pl.BlockSpec(memory_space=pl.ANY),
        out_shape=jax.ShapeDtypeStruct(queries.shape, jnp.bfloat16),
        scratch_shapes=[held, held, pltpu.SemaphoreType.DMA((ch,)), pltpu.SemaphoreType.DMA((ch,))],
        input_output_aliases={1: 0},
        compiler_params=params(8),
        cost_estimate=pl.CostEstimate(
            flops=half * pieces[0].size, bytes_accessed=6 * half * pieces[0].size, transcendentals=0
        ),
        name="half_gate",
    )(place, queries, *pieces)


def step_gate_kernel(place_ref, queries_ref, piece_ref, *refs, first, step, seq):
    out_ref, query, gated, arrive, leave = refs
    ch, count, _, width = piece_ref.shape

    def column(c):
        return pl.ds(pl.multiple_of((c * seq + (place_ref[0] ^ step)) * width, width), width)

    def inward(c):
        source = queries_ref.at[pl.ds(first, count), :, column(c)]
        return pltpu.make_async_copy(source, query.at[c], arrive.at[c])

    def outward(c):
        target = out_ref.at[pl.ds(first, count), :, column(c)]
        return pltpu.make_async_copy(gated.at[c], target, leave.at[c])

    for c in range(ch):
        inward(c).start()
    for c in range(ch):
        inward(c).wait()
        gated[c] = (query[c].astype(jnp.float32) * piece_ref[c].astype(jnp.float32)).astype(jnp.bfloat16)
        outward(c).start()
    for c in range(ch):
        outward(c).wait()


def step_gate(place, queries, piece, first, step, seq):
    held = pltpu.VMEM(piece.shape, jnp.bfloat16)
    semaphores = pltpu.SemaphoreType.DMA(piece.shape[:1])
    return pl.pallas_call(
        functools.partial(step_gate_kernel, first=first, step=step, seq=seq),
        in_specs=[
            pl.BlockSpec(memory_space=pltpu.SMEM),
            pl.BlockSpec(memory_space=pl.ANY),
            pl.BlockSpec(memory_space=pltpu.VMEM),
        ],
        out_specs=pl.BlockSpec(memory_space=pl.ANY),
        out_shape=jax.ShapeDtypeStruct(queries.shape, jnp.bfloat16),
        scratch_shapes=[held, held, semaphores, semaphores],
        input_output_aliases={1: 0},
        compiler_params=params(8),
        cost_estimate=pl.CostEstimate(flops=piece.size, bytes_accessed=6 * piece.size, transcendentals=0),
        name="step_gate",
    )(place, queries, piece)


def swap(pieces):
    count = lax.axis_size("seq")
    return [
        lax.ppermute(piece, "seq", [(source, source ^ step) for source in range(count)]) if step else piece
        for step, piece in enumerate(pieces)
    ]


def spread(whole):
    return lax.all_to_all(whole, "ch", split_axis=0, concat_axis=0, tiled=True)


def vacant_kernel(*refs):
    pass


def vacant(*arrays):
    return pl.pallas_call(
        vacant_kernel,
        out_specs=[pl.BlockSpec(memory_space=pl.ANY)] * len(arrays),
        out_shape=[jax.ShapeDtypeStruct(array.shape, array.dtype) for array in arrays],
        name="vacant",
    )()


def ordered(pieces, order):
    return [pieces[place] for place in order]


def back(pieces, order):
    return [pieces[order.index(place)] for place in range(len(order))]


def staged(times, place, step, *arrays):
    def round_of(_, held):
        return held[0] + 1, *step(held[0], *held[1:])

    return lax.fori_loop(0, times, round_of, (place, *arrays))[1:]


def shards(proj, short_w, long_filter):
    seq, ch = lax.axis_size("seq"), lax.axis_size("ch")
    tap_count, (seq_count, rows) = short_w.shape[0], proj.shape[:2]
    length, groups = long_filter.shape[1], long_filter.shape[0] // seq
    half = seq_count // 2
    place = lax.axis_index("seq").astype(jnp.int32).reshape(1)
    once = jnp.minimum(lax.axis_index("seq") + 1, 1)
    rim = from_behind(proj[:, rows - (tap_count - 1) :], ("seq", "ch"), 1).transpose(0, 2, 1, 3)
    taps = lax.all_gather(short_w, "ch", axis=2, tiled=True)
    turned = proj.transpose(0, 2, 1, 3)
    own = lax.dynamic_slice_in_dim(long_filter, place[0] * groups, groups, 0)
    filters = own.astype(jnp.float32).reshape(groups, 1, length)

    first = products(place, turned, rim, taps, 0, half, seq, ch, tuple(range(1, seq)))
    begun = first[0]

    def second_out(place, *held):
        (second,) = products(place, turned, rim, taps, half, half, seq, ch, after=[begun, place])
        queries = short_queries(turned, rim, taps, ch, after=[place])
        (stays,) = products(place, turned, rim, taps, 0, half, seq, ch, (0,), after=[begun])
        return queries, stays, *split(spread(second))

    shape = jax.ShapeDtypeStruct((seq_count, rows, proj.shape[3]), proj.dtype)
    queries, stays, *second = staged(once, place, second_out, *vacant(shape, begun, begun, *first))
    second_sent = second[0]

    def first_turn(place, *first):
        whole = spread(join(back(first, [1, 3, 2, 0]), after=[place, second_sent]))
        return ordered(long_conv(place, [whole], filters, seq), [1, 3, 2, 0])

    first = back(staged(once, place, first_turn, *ordered(swap([stays, *first]), [1, 3, 2, 0])), [1, 3, 2, 0])
    first_sent = first[0]

    def second_turn(place, *second):
        (second,) = long_conv(place, second, filters, seq, after=[first_sent])
        return split(spread(second))

    second = staged(once, place, second_turn, *swap(second))
    second_back = second[0]

    def first_gate(place, queries, *first):
        return gate(place, queries, [spread(join(first, after=[place, second_back]))], 0, seq), *first

    out = staged(once, place, first_gate, queries, *swap(first))[0]
    second = swap(second)
    out = half_gate(place, out, second[: seq // 2], half, False)
    if second[0].shape[-1] % 128:
        return half_gate(place, out, second[seq // 2 :], half, True)
    for step in range(seq // 2, seq):
        out = step_gate(place, out, second[step], half, step, seq)
    return out


def solution(mesh):
    in_specs = (P(None, ("seq", "ch"), None, None), P(None, None, "ch"), P("ch", None))
    out_specs = P(None, ("seq", "ch"), None)
    return jax.shard_map(shards, mesh=mesh, in_specs=in_specs, out_specs=out_specs, check_vma=False)
```
